256 devices in a mesh: ga: 32 (over y, z), ba: 8 (over x, core).
Axes of the slice: x: 4, y: 4, z: 8, core: 2. Of those that a mesh axis runs over, the one named last changes fastest.
Arguments:
- orbitals: bfloat16 [2, 512, 294912], P(None, 'ga', 'ba'), may hold values from -24 to 24, as said below
- exchange_applied: bfloat16 [2, 512, 294912], P(None, 'ga', 'ba'), may hold values from -48 to 48, as said below
Outputs:
- projectors: float32 [2, 512, 294912], P(None, None, ('ba', 'ga'))
The draws below stay inside these ranges and needn't reach their ends.
Inputs may be any that keep to these rules, and one draw needn't show every extreme that they name: orbitals are bounded. exchange_applied is bounded and gram is positive definite.
All inputs are finite; a program needn't handle non-finite values.
Results may differ from the reference program's by a relative error of at most 0.0003.
Values may be sent and summed in bfloat16 or wider, within the bound.
A program may use at most 128 MiB of HBM per device.

```python
import jax
import jax.numpy as jnp
from jax import lax

NB = 512
NG = 294912
SETS = 2


def shared_fields(key):
    field_key = jax.random.fold_in(key, 21)
    coeff_key = jax.random.fold_in(key, 22)
    weight_key = jax.random.fold_in(key, 24)
    signs_key = jax.random.fold_in(key, 25)
    base = jnp.clip(jax.random.normal(field_key, (SETS, NB, NG), jnp.float32), -6.0, 6.0)
    mixed = base
    offsets = (1, 3, NB // 8 + 1, NB // 2 - 5)
    for index in range(4):
        magnitude = jax.random.uniform(jax.random.fold_in(coeff_key, index), (SETS, NB, 1), jnp.float32, 0.08, 0.18)
        signs = 2.0 * jax.random.randint(jax.random.fold_in(signs_key, index), (SETS, NB, 1), 0, 2).astype(jnp.float32) - 1.0
        mixed = mixed + magnitude * signs * jnp.roll(base, offsets[index], axis=1)
    orbit = jnp.clip(mixed, -24.0, 24.0)
    weight = jnp.exp(jnp.log(0.5) + jnp.log(4.0) * jax.random.uniform(weight_key, (1, 1, NG), jnp.float32))
    return (orbit, weight)


def draw_orbitals(key, part):
    orbit, weight = shared_fields(key)
    return orbit.astype(jnp.bfloat16)


def draw_exchange_applied(key, part):
    orbit, weight = shared_fields(key)
    return (-(orbit * weight)).astype(jnp.bfloat16)


def setup_inputs(seed: int = 0) -> dict:
    key_list = jax.random.split(jax.random.key(seed), 3)
    orbitals = draw_orbitals(jax.random.fold_in(key_list[2], 71), 0)
    exchange_applied = draw_exchange_applied(jax.random.fold_in(key_list[2], 71), 0)
    return dict(orbitals=orbitals, exchange_applied=exchange_applied)


def one_set(pair):
    orbit, applied = pair
    correlation = jnp.dot(orbit.astype(jnp.float32), applied.T.astype(jnp.float32), preferred_element_type=jnp.float32)
    gram = -(correlation + correlation.T) / (2.0 * NG)
    lower = jnp.linalg.cholesky(gram)
    eye = jnp.eye(lower.shape[0], dtype=lower.dtype)
    inverse = jax.scipy.linalg.solve_triangular(lower, eye, lower=True)
    return jnp.dot(inverse, applied.astype(inverse.dtype), precision=lax.Precision.HIGHEST)

def reference(orbitals, exchange_applied):
    return lax.map(one_set, (orbitals, exchange_applied))
```

```python
import functools

import jax
import jax.numpy as jnp
from jax import lax
from jax.experimental import pallas as pl
from jax.experimental.pallas import tpu as pltpu
from jax.sharding import PartitionSpec as P

MESH = pl.DeviceIdType.MESH
HIGHEST = lax.Precision.HIGHEST
F32 = jnp.float32
BF16 = jnp.bfloat16
NB, NG, SETS = 512, 294912, 2
BLK = 128
NBLK = NB // BLK
PANEL = 16
PAIRS = [(i, j) for i in range(NBLK) for j in range(i, NBLK)]
FIRST = [PAIRS.index((i, i)) for i in range(NBLK)]
GROWS = len(PAIRS) * BLK
VMEM_LIMIT = 60 * 2**20
YS, ZS = 4, 8


def ring(d, n):
    return min(d, n - d)


OFFSETS = sorted(
    [(dy, dz) for dy in range(YS) for dz in range(ZS) if (dy, dz) != (0, 0)],
    key=lambda t: ring(t[0], YS) + ring(t[1], ZS),
)


def tn(a, b):
    return lax.dot_general(a, b, (((0,), (0,)), ((), ())), precision=HIGHEST, preferred_element_type=F32)


def nn(a, b):
    return lax.dot_general(a, b, (((1,), (0,)), ((), ())), precision=HIGHEST, preferred_element_type=F32)


def nt(a, b):
    return lax.dot_general(a, b, (((1,), (1,)), ((), ())), preferred_element_type=F32)


def factor_block(a_ref, x_ref):
    rows = lax.broadcasted_iota(jnp.int32, (BLK, BLK), 0)
    cols = lax.broadcasted_iota(jnp.int32, (BLK, BLK), 1)
    x_ref[...] = jnp.where(rows == cols, 1.0, 0.0).astype(F32)
    sub = lax.broadcasted_iota(jnp.int32, (8, BLK), 0)
    wide = (8, BLK)
    own = PANEL // 8
    for base in range(0, BLK, PANEL):
        v = own if base + PANEL == BLK else 2 * own
        a = [a_ref[base + 8 * i : base + 8 * i + 8, :] for i in range(v)]
        x = [x_ref[base + 8 * i : base + 8 * i + 8, :] for i in range(v)]
        c = [[jnp.broadcast_to(a[i][:, base + r : base + r + 1], wide) for i in range(v)] for r in range(PANEL)]
        d = [jnp.ones(wide, F32) for _ in range(own)]
        for r in range(PANEL):
            h, q = divmod(r, 8)
            pivot = jnp.broadcast_to(c[r][h][q : q + 1, :], wide)
            inv = 1.0 / pivot
            d[h] = jnp.where(sub == q, pivot, d[h])
            arow = jnp.broadcast_to(a[h][q : q + 1, :], wide)
            xrow = jnp.broadcast_to(x[h][q : q + 1, :], wide)
            crow = {j: jnp.broadcast_to(c[j][h][q : q + 1, :], wide) for j in range(r + 1, PANEL)}
            for i in range(h, v):
                if i == h and q == 7:
                    continue
                m = c[r][i] * inv
                if i == h:
                    m = jnp.where(sub > q, m, 0.0)
                for j in range(r + 1, PANEL):
                    c[j][i] = c[j][i] - m * crow[j]
                a[i] = a[i] - m * arow
                x[i] = x[i] - m * xrow
        for i in range(own):
            s = lax.rsqrt(d[i])
            a[i] = a[i] * s
            x[i] = x[i] * s
        for i in range(v):
            a_ref[base + 8 * i : base + 8 * i + 8, :] = a[i]
            x_ref[base + 8 * i : base + 8 * i + 8, :] = x[i]
        rest = base + 2 * PANEL
        if rest < BLK:
            u = a_ref[base : base + PANEL, :]
            w = x_ref[base : base + PANEL, :]
            a_ref[rest:, :] = a_ref[rest:, :] - tn(u, u)[rest:, :]
            x_ref[rest:, :] = x_ref[rest:, :] - tn(u, w)[rest:, :]


def factor(g_ref, x_ref, a_ref, m_ref, u_ref):
    def block(i, j):
        at = (FIRST[i] + j - i) * BLK
        return slice(at, at + BLK)

    x_ref[...] = jnp.zeros((NB, NB), F32)
    for k in range(NBLK):
        lo, hi = BLK * k, BLK * k + BLK
        a_ref[...] = g_ref[block(k, k), :]
        factor_block(a_ref, m_ref)
        m = m_ref[...]
        if k:
            x_ref[lo:hi, :lo] = nn(m, x_ref[lo:hi, :lo])
        x_ref[lo:hi, lo:hi] = m
        for j in range(k + 1, NBLK):
            u_ref[:, j * BLK : (j + 1) * BLK] = nn(m, g_ref[block(k, j), :])
        for i in range(k + 1, NBLK):
            li = BLK * i
            ui = u_ref[:, li : li + BLK]
            update = tn(ui, u_ref[:, li:])
            for j in range(i, NBLK):
                g_ref[block(i, j), :] = g_ref[block(i, j), :] - update[:, (j - i) * BLK : (j - i + 1) * BLK]
            x_ref[li : li + BLK, :hi] = x_ref[li : li + BLK, :hi] - tn(ui, x_ref[lo:hi, :hi])


def exchange_kernel(o_ref, w_ref, g_out, w_out, o_slab, send_sem, recv_sem, own_sem):
    ga, ba = lax.axis_index("ga"), lax.axis_index("ba")
    y, z = ga // ZS, lax.rem(ga, ZS)
    peers = [lax.rem(y + dy, YS) * ZS + lax.rem(z + dz, ZS) for dy, dz in OFFSETS]
    barrier = pltpu.get_barrier_semaphore()
    for p in peers:
        pl.semaphore_signal(barrier, inc=1, device_id=(p, ba), device_id_type=MESH)
    width = o_slab.shape[2]
    rows = o_ref.shape[1]
    mine = pl.ds(pl.multiple_of(ga * rows, rows), rows)
    own = pl.ds(pl.multiple_of(ga * width, BLK), width)
    arrays = ((o_ref, o_slab), (w_ref, w_out))
    local = [
        pltpu.make_async_copy(src.at[s, :, own], dst.at[s, mine, :], own_sem.at[s, a])
        for s in range(SETS)
        for a, (src, dst) in enumerate(arrays)
    ]
    for copy in local:
        copy.start()
    pl.semaphore_wait(barrier, len(peers))
    for s in range(SETS):
        for p in peers:
            columns = pl.ds(pl.multiple_of(p * width, BLK), width)
            for a, (src, dst) in enumerate(arrays):
                pltpu.make_async_remote_copy(
                    src_ref=src.at[s, :, columns],
                    dst_ref=dst.at[s, mine, :],
                    send_sem=send_sem.at[s, a],
                    recv_sem=recv_sem.at[s, a],
                    device_id=(p, ba),
                    device_id_type=MESH,
                ).start()
    for copy in local:
        copy.wait()
    for s in range(SETS):
        for a, (src, dst) in enumerate(arrays):
            all_but_one = dst.at[s, pl.ds(0, len(peers) * rows), :]
            pltpu.make_async_copy(all_but_one, all_but_one, recv_sem.at[s, a]).wait()
        for i in range(NBLK):
            lo = BLK * i
            product = nt(o_slab[s, lo : lo + BLK, :], w_out[s, lo:, :]) + nt(w_out[s, lo : lo + BLK, :], o_slab[s, lo:, :])
            for j in range(i, NBLK):
                at = (FIRST[i] + j - i) * BLK
                g_out[s, at : at + BLK, :] = product[:, (j - i) * BLK : (j - i + 1) * BLK] * (-0.5 / NG)
    for s in range(SETS):
        for a, (src, dst) in enumerate(arrays):
            all_but_one = dst.at[s, pl.ds(0, len(peers) * rows), :]
            pltpu.make_async_copy(all_but_one, all_but_one, send_sem.at[s, a]).wait()


def finish_kernel(g_ref, w_ref, out_ref, g, x, a, m, u):
    def one_set(s, carry):
        g[...] = g_ref[s]
        factor(g, x, a, m, u)
        for i in range(NBLK):
            lo, hi = BLK * i, BLK * i + BLK
            inverse = x[lo:hi, :hi]
            head = inverse.astype(BF16)
            tail = (inverse - head.astype(F32)).astype(BF16)
            slab = w_ref[s, :hi, :]
            out_ref[s, lo:hi, :] = jnp.dot(head, slab, preferred_element_type=F32) + jnp.dot(
                tail, slab, preferred_element_type=F32
            )
        return carry

    lax.fori_loop(0, SETS, one_set, 0)


def per_device(orbitals, exchange_applied):
    width = orbitals.shape[2] // (YS * ZS)
    vmem = pl.BlockSpec(memory_space=pltpu.VMEM)
    anywhere = pl.BlockSpec(memory_space=pl.ANY)
    gram, slab = pl.pallas_call(
        exchange_kernel,
        out_shape=(
            jax.ShapeDtypeStruct((SETS, GROWS, BLK), F32),
            jax.ShapeDtypeStruct((SETS, NB, width), BF16),
        ),
        in_specs=[anywhere, anywhere],
        out_specs=(vmem, vmem),
        scratch_shapes=[
            pltpu.VMEM((SETS, NB, width), BF16),
            pltpu.SemaphoreType.DMA((SETS, 2)),
            pltpu.SemaphoreType.DMA((SETS, 2)),
            pltpu.SemaphoreType.DMA((SETS, 2)),
        ],
        compiler_params=pltpu.CompilerParams(collective_id=0, has_side_effects=True, vmem_limit_bytes=VMEM_LIMIT),
    )(orbitals, exchange_applied)
    gram = lax.psum(gram, ("ga", "ba"))
    return pl.pallas_call(
        finish_kernel,
        out_shape=jax.ShapeDtypeStruct((SETS, NB, width), F32),
        in_specs=[vmem, vmem],
        out_specs=vmem,
        scratch_shapes=[
            pltpu.VMEM((GROWS, BLK), F32),
            pltpu.VMEM((NB, NB), F32),
            pltpu.VMEM((BLK, BLK), F32),
            pltpu.VMEM((BLK, BLK), F32),
            pltpu.VMEM((BLK, NB), F32),
        ],
        compiler_params=pltpu.CompilerParams(vmem_limit_bytes=VMEM_LIMIT),
    )(gram, slab)


def solution(mesh):
    placed = (P(None, "ga", "ba"), P(None, "ga", "ba"))
    return jax.shard_map(
        per_device,
        mesh=mesh,
        in_specs=placed,
        out_specs=P(None, None, ("ba", "ga")),
        check_vma=False,
    )
```

```python
import functools

import jax
import jax.numpy as jnp
from jax import lax
from jax.experimental import pallas as pl
from jax.experimental.pallas import tpu as pltpu
from jax.sharding import PartitionSpec as P

MESH = pl.DeviceIdType.MESH
HIGHEST = lax.Precision.HIGHEST
F32 = jnp.float32
BF16 = jnp.bfloat16
NB, NG, SETS = 512, 294912, 2
BLK = 128
NBLK = NB // BLK
PANEL = 16
PAIRS = [(i, j) for i in range(NBLK) for j in range(i, NBLK)]
FIRST = [PAIRS.index((i, i)) for i in range(NBLK)]
GROWS = 12 * BLK
XS, YS, ZS = 4, 4, 8
HALF = GROWS // 2
PART = HALF // 2 // XS
CHUNK = 2 * PART // ZS
VMEM_LIMIT = 60 * 2**20

def ring(d, n):
    return min(d, n - d)


OFFSETS = sorted(
    [(dy, dz) for dy in range(YS) for dz in range(ZS) if (dy, dz) != (0, 0)],
    key=lambda t: ring(t[0], YS) + ring(t[1], ZS),
)


def tn(a, b):
    return lax.dot_general(a, b, (((0,), (0,)), ((), ())), precision=HIGHEST, preferred_element_type=F32)


def nn(a, b):
    return lax.dot_general(a, b, (((1,), (0,)), ((), ())), precision=HIGHEST, preferred_element_type=F32)


def nt(a, b):
    return lax.dot_general(a, b, (((1,), (1,)), ((), ())), preferred_element_type=F32)


def factor_block(a_ref, x_ref):
    rows = lax.broadcasted_iota(jnp.int32, (BLK, BLK), 0)
    cols = lax.broadcasted_iota(jnp.int32, (BLK, BLK), 1)
    x_ref[...] = jnp.where(rows == cols, 1.0, 0.0).astype(F32)
    sub = lax.broadcasted_iota(jnp.int32, (8, BLK), 0)
    wide = (8, BLK)
    own = PANEL // 8
    for base in range(0, BLK, PANEL):
        v = own if base + PANEL == BLK else 2 * own
        a = [a_ref[base + 8 * i : base + 8 * i + 8, :] for i in range(v)]
        x = [x_ref[base + 8 * i : base + 8 * i + 8, :] for i in range(v)]
        c = [[jnp.broadcast_to(a[i][:, base + r : base + r + 1], wide) for i in range(v)] for r in range(PANEL)]
        d = [jnp.ones(wide, F32) for _ in range(own)]
        for r in range(PANEL):
            h, q = divmod(r, 8)
            pivot = jnp.broadcast_to(c[r][h][q : q + 1, :], wide)
            inv = 1.0 / pivot
            d[h] = jnp.where(sub == q, pivot, d[h])
            arow = jnp.broadcast_to(a[h][q : q + 1, :], wide)
            xrow = jnp.broadcast_to(x[h][q : q + 1, :], wide)
            crow = {j: jnp.broadcast_to(c[j][h][q : q + 1, :], wide) for j in range(r + 1, PANEL)}
            for i in range(h, v):
                if i == h and q == 7:
                    continue
                m = c[r][i] * inv
                if i == h:
                    m = jnp.where(sub > q, m, 0.0)
                for j in range(r + 1, PANEL):
                    c[j][i] = c[j][i] - m * crow[j]
                a[i] = a[i] - m * arow
                x[i] = x[i] - m * xrow
        for i in range(own):
            s = lax.rsqrt(d[i])
            a[i] = a[i] * s
            x[i] = x[i] * s
        for i in range(v):
            a_ref[base + 8 * i : base + 8 * i + 8, :] = a[i]
            x_ref[base + 8 * i : base + 8 * i + 8, :] = x[i]
        rest = base + 2 * PANEL
        if rest < BLK:
            u = a_ref[base : base + PANEL, :]
            w = x_ref[base : base + PANEL, :]
            a_ref[rest:, :] = a_ref[rest:, :] - tn(u, u)[rest:, :]
            x_ref[rest:, :] = x_ref[rest:, :] - tn(u, w)[rest:, :]


def factor(g_ref, x_ref, a_ref, m_ref, u_ref):
    def block(i, j):
        at = (FIRST[i] + j - i) * BLK
        return slice(at, at + BLK)

    x_ref[...] = jnp.zeros((NB, NB), F32)
    for k in range(NBLK):
        lo, hi = BLK * k, BLK * k + BLK
        a_ref[...] = g_ref[block(k, k), :]
        factor_block(a_ref, m_ref)
        m = m_ref[...]
        if k:
            x_ref[lo:hi, :lo] = nn(m, x_ref[lo:hi, :lo])
        x_ref[lo:hi, lo:hi] = m
        for j in range(k + 1, NBLK):
            u_ref[:, j * BLK : (j + 1) * BLK] = nn(m, g_ref[block(k, j), :])
        for i in range(k + 1, NBLK):
            li = BLK * i
            ui = u_ref[:, li : li + BLK]
            update = tn(ui, u_ref[:, li:])
            for j in range(i, NBLK):
                g_ref[block(i, j), :] = g_ref[block(i, j), :] - update[:, (j - i) * BLK : (j - i + 1) * BLK]
            x_ref[li : li + BLK, :hi] = x_ref[li : li + BLK, :hi] - tn(ui, x_ref[lo:hi, :hi])


def exchange_kernel(
    o_ref, w_ref, g_out, w_out, o_slab, part, half, from_x, from_y, third, from_z, fourth, from_4, send_sem, recv_sem, own_sem, out_sem, in_sem
):
    ga, ba = lax.axis_index("ga"), lax.axis_index("ba")
    y, z = ga // ZS, lax.rem(ga, ZS)
    x, core = ba // 2, lax.rem(ba, 2)

    def device(x, y, z, core):
        return (y * ZS + z, x * 2 + core)

    def ahead(i, k, n):
        return lax.rem(i + k, n)

    peers = [device(x, ahead(y, dy, YS), ahead(z, dz, ZS), core) for dy, dz in OFFSETS]
    partner = device(x, y, z, 1 - core)
    beside = [device(ahead(x, k, XS), y, z, core) for k in range(1, XS)]
    barrier = pltpu.get_barrier_semaphore()
    for p in [*peers, partner, *beside]:
        pl.semaphore_signal(barrier, inc=1, device_id=p, device_id_type=MESH)
    width = o_slab.shape[2]
    rows = o_ref.shape[1]
    mine = pl.ds(pl.multiple_of(ga * rows, rows), rows)
    own = pl.ds(pl.multiple_of(ga * width, BLK), width)
    arrays = ((o_ref, o_slab), (w_ref, w_out))
    local = [
        pltpu.make_async_copy(src.at[s, :, own], dst.at[s, mine, :], own_sem.at[s, a])
        for s in range(SETS)
        for a, (src, dst) in enumerate(arrays)
    ]
    for copy in local:
        copy.start()
    part[:, len(PAIRS) * BLK :, :] = jnp.zeros((SETS, GROWS - len(PAIRS) * BLK, BLK), F32)
    pl.semaphore_wait(barrier, len(peers) + 1 + len(beside))

    def send_slabs(s, chosen):
        for p in chosen:
            columns = pl.ds(pl.multiple_of(p[0] * width, BLK), width)
            for a, (src, dst) in enumerate(arrays):
                pltpu.make_async_remote_copy(
                    src_ref=src.at[s, :, columns],
                    dst_ref=dst.at[s, mine, :],
                    send_sem=send_sem.at[s, a],
                    recv_sem=recv_sem.at[s, a],
                    device_id=p,
                    device_id_type=MESH,
                ).start()

    def wait_slabs(s, sem):
        for a, (src, dst) in enumerate(arrays):
            all_but_one = dst.at[s, pl.ds(0, len(peers) * rows), :]
            pltpu.make_async_copy(all_but_one, all_but_one, sem.at[s, a]).wait()

    def correlate(s):
        for i in range(NBLK):
            lo = BLK * i
            product = nt(o_slab[s, lo : lo + BLK, :], w_out[s, lo:, :]) + nt(w_out[s, lo : lo + BLK, :], o_slab[s, lo:, :])
            for j in range(i, NBLK):
                at = (FIRST[i] + j - i) * BLK
                part[s, at : at + BLK, :] = product[:, (j - i) * BLK : (j - i + 1) * BLK] * (-0.5 / NG)

    def span(start, size):
        return pl.ds(pl.multiple_of(start, 8), size)

    def total(s, between):
        used = []

        def stage(t, transfers):
            copies = []
            for src, dst, to in transfers:
                at = len(used) + len(copies)
                copies.append(
                    pltpu.make_async_remote_copy(
                        src_ref=src, dst_ref=dst, send_sem=out_sem.at[s, at], recv_sem=in_sem.at[s, at], device_id=to, device_id_type=MESH
                    )
                )
            for copy in copies:
                copy.start()
            between(t)
            for copy in copies:
                copy.wait_recv()
            used.extend(copies)

        stage(0, [(part.at[s, span((1 - core) * HALF, HALF), :], half.at[s], partner)])
        half[s] = half[s] + part[s, span(core * HALF, HALF), :]
        side = HALF // 2
        xs = [ahead(x, k, XS) for k in range(1, XS)]
        ys = [ahead(y, k, YS) for k in range(1, YS)]
        zs = [ahead(z, k, ZS) for k in range(1, ZS)]
        stage(
            1,
            [(half.at[s, span(xx * PART, PART), :], from_x.at[s, k], device(xx, y, z, core)) for k, xx in enumerate(xs)]
            + [(half.at[s, span(side + yy * PART, PART), :], from_y.at[s, k], device(x, yy, z, core)) for k, yy in enumerate(ys)],
        )
        third[s, :PART, :] = half[s, span(x * PART, PART), :] + (from_x[s, 0] + from_x[s, 1] + from_x[s, 2])
        third[s, PART:, :] = half[s, span(side + y * PART, PART), :] + (from_y[s, 0] + from_y[s, 1] + from_y[s, 2])
        stage(2, [(third.at[s, span(zz * CHUNK, CHUNK), :], from_z.at[s, k], device(x, y, zz, core)) for k, zz in enumerate(zs)])
        got = [from_z[s, k] for k in range(ZS - 1)]
        fourth[s] = third[s, span(z * CHUNK, CHUNK), :] + (
            ((got[0] + got[1]) + (got[2] + got[3])) + ((got[4] + got[5]) + got[6])
        )
        upper = z // (ZS // 2)
        stage(
            3,
            [
                (fourth.at[s], from_4.at[s, k - 1], device(ahead(x, k * upper, XS), ahead(y, k * (1 - upper), YS), z, core))
                for k in range(1, 4)
            ],
        )
        start_x = core * HALF + x * PART
        start_y = core * HALF + side + y * PART
        start = (1 - upper) * (start_x + z * CHUNK) + upper * (start_y + (z - ZS // 2) * CHUNK)
        g_out[s, span(start, CHUNK), :] = fourth[s] + (from_4[s, 0] + from_4[s, 1] + from_4[s, 2])
        here = g_out.at[s, span(start, CHUNK), :]
        stage(4, [(here, here, device(x, y, zz, core)) for zz in zs])
        along_x = g_out.at[s, span(start_x, PART), :]
        along_y = g_out.at[s, span(start_y, PART), :]
        stage(
            5,
            [(along_x, along_x, device(xx, y, z, core)) for xx in xs] + [(along_y, along_y, device(x, yy, z, core)) for yy in ys],
        )
        share = g_out.at[s, span(core * HALF, HALF), :]
        stage(6, [(share, share, partner)])
        return used

    batches = [peers[i::8] for i in range(8)]
    send_slabs(0, peers)
    send_slabs(1, batches[0])
    for copy in local:
        copy.wait()
    wait_slabs(0, recv_sem)
    correlate(0)
    used = total(0, lambda t: send_slabs(1, batches[t + 1]))
    wait_slabs(1, recv_sem)
    correlate(1)
    used = used + total(1, lambda t: None)
    for copy in used:
        copy.wait_send()
    for s in range(SETS):
        wait_slabs(s, send_sem)


def finish_kernel(g_ref, w_ref, out_ref, g, x, a, m, u):
    def one_set(s, carry):
        g[...] = g_ref[s]
        factor(g, x, a, m, u)
        for i in range(NBLK):
            lo, hi = BLK * i, BLK * i + BLK
            inverse = x[lo:hi, :hi]
            head = inverse.astype(BF16)
            tail = (inverse - head.astype(F32)).astype(BF16)
            slab = w_ref[s, :hi, :]
            out_ref[s, lo:hi, :] = jnp.dot(head, slab, preferred_element_type=F32) + jnp.dot(
                tail, slab, preferred_element_type=F32
            )
        return carry

    lax.fori_loop(0, SETS, one_set, 0)


def per_device(orbitals, exchange_applied):
    width = orbitals.shape[2] // (YS * ZS)
    vmem = pl.BlockSpec(memory_space=pltpu.VMEM)
    anywhere = pl.BlockSpec(memory_space=pl.ANY)
    gram, slab = pl.pallas_call(
        exchange_kernel,
        out_shape=(
            jax.ShapeDtypeStruct((SETS, GROWS, BLK), F32),
            jax.ShapeDtypeStruct((SETS, NB, width), BF16),
        ),
        in_specs=[anywhere, anywhere],
        out_specs=(vmem, vmem),
        scratch_shapes=[
            pltpu.VMEM((SETS, NB, width), BF16),
            pltpu.VMEM((SETS, GROWS, BLK), F32),
            pltpu.VMEM((SETS, HALF, BLK), F32),
            pltpu.VMEM((SETS, XS - 1, PART, BLK), F32),
            pltpu.VMEM((SETS, YS - 1, PART, BLK), F32),
            pltpu.VMEM((SETS, 2 * PART, BLK), F32),
            pltpu.VMEM((SETS, ZS - 1, CHUNK, BLK), F32),
            pltpu.VMEM((SETS, CHUNK, BLK), F32),
            pltpu.VMEM((SETS, 3, CHUNK, BLK), F32),
            pltpu.SemaphoreType.DMA((SETS, 2)),
            pltpu.SemaphoreType.DMA((SETS, 2)),
            pltpu.SemaphoreType.DMA((SETS, 2)),
            pltpu.SemaphoreType.DMA((SETS, 31)),
            pltpu.SemaphoreType.DMA((SETS, 31)),
        ],
        compiler_params=pltpu.CompilerParams(collective_id=0, has_side_effects=True, vmem_limit_bytes=VMEM_LIMIT),
    )(orbitals, exchange_applied)
    return pl.pallas_call(
        finish_kernel,
        out_shape=jax.ShapeDtypeStruct((SETS, NB, width), F32),
        in_specs=[vmem, vmem],
        out_specs=vmem,
        scratch_shapes=[
            pltpu.VMEM((GROWS, BLK), F32),
            pltpu.VMEM((NB, NB), F32),
            pltpu.VMEM((BLK, BLK), F32),
            pltpu.VMEM((BLK, BLK), F32),
            pltpu.VMEM((BLK, NB), F32),
        ],
        compiler_params=pltpu.CompilerParams(vmem_limit_bytes=VMEM_LIMIT),
    )(gram, slab)


def solution(mesh):
    placed = (P(None, "ga", "ba"), P(None, "ga", "ba"))
    return jax.shard_map(
        per_device,
        mesh=mesh,
        in_specs=placed,
        out_specs=P(None, None, ("ba", "ga")),
        check_vma=False,
    )
```

```python
import functools

import jax
import jax.numpy as jnp
from jax import lax
from jax.experimental import pallas as pl
from jax.experimental.pallas import tpu as pltpu
from jax.sharding import PartitionSpec as P

MESH = pl.DeviceIdType.MESH
HIGHEST = lax.Precision.HIGHEST
F32 = jnp.float32
BF16 = jnp.bfloat16
NB, NG, SETS = 512, 294912, 2
BLK = 128
HB = BLK // 2
NBLK = NB // BLK
PANEL = 16
PAIRS = [(i, j) for i in range(NBLK) for j in range(i, NBLK)]
FIRST = [PAIRS.index((i, i)) for i in range(NBLK)]
GROWS = 12 * BLK
XS, YS, ZS = 4, 4, 8
HALF = GROWS // 2
PART = HALF // 2 // XS
CHUNK = 2 * PART // ZS
VMEM_LIMIT = 60 * 2**20

def ring(d, n):
    return min(d, n - d)


OFFSETS = sorted(
    [(dy, dz) for dy in range(YS) for dz in range(ZS) if (dy, dz) != (0, 0)],
    key=lambda t: ring(t[0], YS) + ring(t[1], ZS),
)


def tn(a, b):
    return lax.dot_general(a, b, (((0,), (0,)), ((), ())), precision=HIGHEST, preferred_element_type=F32)


def nn(a, b):
    return lax.dot_general(a, b, (((1,), (0,)), ((), ())), precision=HIGHEST, preferred_element_type=F32)


def nt(a, b):
    return lax.dot_general(a, b, (((1,), (1,)), ((), ())), preferred_element_type=F32)


def pack(first, second):
    return jnp.concatenate([first[:, :HB], second[:, :HB], first[:, HB:], second[:, HB:]], axis=1)


def unpack(packed):
    return (
        jnp.concatenate([packed[:, :HB], packed[:, BLK : BLK + HB]], axis=1),
        jnp.concatenate([packed[:, HB:BLK], packed[:, BLK + HB :]], axis=1),
    )


def factor_blocks(a_ref, x_ref):
    wide = (8, BLK)
    sub = lax.broadcasted_iota(jnp.int32, wide, 0)
    left = lax.broadcasted_iota(jnp.int32, wide, 1) < HB
    rows = lax.broadcasted_iota(jnp.int32, (BLK, 2 * BLK), 0)
    cols = lax.broadcasted_iota(jnp.int32, (BLK, 2 * BLK), 1)
    x_ref[...] = jnp.where(rows == cols % HB + cols // BLK * HB, 1.0, 0.0).astype(F32)
    own = PANEL // 8
    for base in range(0, BLK, PANEL):
        v = own if base + PANEL == BLK else 2 * own
        at = [slice(base + 8 * i, base + 8 * i + 8) for i in range(v)]
        t = [[a_ref[at[i], :BLK], a_ref[at[i], BLK:], x_ref[at[i], :BLK], x_ref[at[i], BLK:]] for i in range(v)]
        side, first = divmod(base, HB)
        c = [
            [
                jnp.where(
                    left,
                    jnp.broadcast_to(t[i][side][:, first + r : first + r + 1], wide),
                    jnp.broadcast_to(t[i][side][:, HB + first + r : HB + first + r + 1], wide),
                )
                for i in range(v)
            ]
            for r in range(PANEL)
        ]
        live = [k for k in range(4) if not (k == 0 and side == 1) and not (k == 3 and side == 0 and base + 2 * PANEL <= HB)]
        d = [jnp.ones(wide, F32) for _ in range(own)]
        for r in range(PANEL):
            h, q = divmod(r, 8)
            pivot = jnp.broadcast_to(c[r][h][q : q + 1, :], wide)
            inv = 1.0 / pivot
            d[h] = jnp.where(sub == q, pivot, d[h])
            trow = {k: jnp.broadcast_to(t[h][k][q : q + 1, :], wide) for k in live}
            crow = {j: jnp.broadcast_to(c[j][h][q : q + 1, :], wide) for j in range(r + 1, PANEL)}
            for i in range(h, v):
                if i == h and q == 7:
                    continue
                m = c[r][i] * inv
                if i == h:
                    m = jnp.where(sub > q, m, 0.0)
                for j in range(r + 1, PANEL):
                    c[j][i] = c[j][i] - m * crow[j]
                for k in live:
                    t[i][k] = t[i][k] - m * trow[k]
        for i in range(own):
            s = lax.rsqrt(d[i])
            t[i] = [e * s for e in t[i]]
        for i in range(v):
            a_ref[at[i], :BLK], a_ref[at[i], BLK:], x_ref[at[i], :BLK], x_ref[at[i], BLK:] = t[i]
        rest = base + 2 * PANEL
        if rest < BLK:
            u = a_ref[base : base + PANEL, :]
            w = x_ref[base : base + PANEL, :]
            both = jnp.concatenate([u, w], axis=1)
            for lo in (0, HB):
                if rest >= lo + HB:
                    continue
                skip = max(rest - lo, 0)
                p = tn(u[:, 2 * lo : 2 * lo + BLK], both)
                pick = lax.broadcasted_iota(jnp.int32, (HB - skip, 4 * BLK), 1) % BLK < HB
                update = jnp.where(pick, p[skip:HB], p[HB + skip :])
                if lo == 0 or rest <= HB:
                    a_ref[lo + skip : lo + HB, :] = a_ref[lo + skip : lo + HB, :] - update[:, : 2 * BLK]
                else:
                    a_ref[lo + skip : lo + HB, BLK:] = a_ref[lo + skip : lo + HB, BLK:] - update[:, BLK : 2 * BLK]
                x_ref[lo + skip : lo + HB, :] = x_ref[lo + skip : lo + HB, :] - update[:, 2 * BLK :]


def factor(g_ref, x_ref, a_ref, m_ref, u_ref):
    def block(i, j):
        at = (FIRST[i] + j - i) * BLK
        return slice(at, at + BLK)

    x_ref[...] = jnp.zeros((SETS, NB, NB), F32)

    def step(k, carry):
        diagonal = pl.ds(pl.multiple_of(k * (2 * NBLK + 1 - k) // 2 * BLK, BLK), BLK)
        a_ref[...] = pack(g_ref[0, diagonal, :], g_ref[1, diagonal, :])
        factor_blocks(a_ref, m_ref)
        ms = unpack(m_ref[...])
        for kk in range(NBLK):
            @pl.when(k == kk)
            def _():
                lo, hi = BLK * kk, BLK * kk + BLK
                for s, m in enumerate(ms):
                    if kk:
                        x_ref[s, lo:hi, :lo] = nn(m, x_ref[s, lo:hi, :lo])
                    x_ref[s, lo:hi, lo:hi] = m
                    for j in range(kk + 1, NBLK):
                        u_ref[s, :, j * BLK : (j + 1) * BLK] = nn(m, g_ref[s, block(kk, j), :])
                for s, m in enumerate(ms):
                    for i in range(kk + 1, NBLK):
                        li = BLK * i
                        ui = u_ref[s, :, li : li + BLK]
                        update = tn(ui, u_ref[s, :, li:])
                        for j in range(i, NBLK):
                            g_ref[s, block(i, j), :] = g_ref[s, block(i, j), :] - update[:, (j - i) * BLK : (j - i + 1) * BLK]
                        x_ref[s, li : li + BLK, :hi] = x_ref[s, li : li + BLK, :hi] - tn(ui, x_ref[s, lo:hi, :hi])
        return carry

    lax.fori_loop(0, NBLK, step, 0)


def exchange_kernel(
    o_ref, w_ref, g_out, w_out, o_slab, w_slab, part, half, from_x, from_y, third, from_z, fourth, from_4, send_sem, recv_sem, own_sem, out_sem, in_sem, keep_sem
):
    ga, ba = lax.axis_index("ga"), lax.axis_index("ba")
    y, z = ga // ZS, lax.rem(ga, ZS)
    x, core = ba // 2, lax.rem(ba, 2)

    def device(x, y, z, core):
        return (y * ZS + z, x * 2 + core)

    def ahead(i, k, n):
        return lax.rem(i + k, n)

    peers = [device(x, ahead(y, dy, YS), ahead(z, dz, ZS), core) for dy, dz in OFFSETS]
    partner = device(x, y, z, 1 - core)
    beside = [device(ahead(x, k, XS), y, z, core) for k in range(1, XS)]
    barrier = pltpu.get_barrier_semaphore()
    for p in [*peers, partner, *beside]:
        pl.semaphore_signal(barrier, inc=1, device_id=p, device_id_type=MESH)
    width = o_slab.shape[2]
    rows = o_ref.shape[1]
    mine = pl.ds(pl.multiple_of(ga * rows, rows), rows)
    own = pl.ds(pl.multiple_of(ga * width, BLK), width)
    arrays = ((o_ref, o_slab), (w_ref, w_slab))
    local = [
        pltpu.make_async_copy(src.at[s, :, own], dst.at[s, mine, :], own_sem.at[s, a])
        for s in range(SETS)
        for a, (src, dst) in enumerate(arrays)
    ]
    for copy in local:
        copy.start()
    part[:, len(PAIRS) * BLK :, :] = jnp.zeros((SETS, GROWS - len(PAIRS) * BLK, BLK), F32)
    pl.semaphore_wait(barrier, len(peers) + 1 + len(beside))

    def send_slabs(s, chosen):
        for p in chosen:
            columns = pl.ds(pl.multiple_of(p[0] * width, BLK), width)
            for a, (src, dst) in enumerate(arrays):
                pltpu.make_async_remote_copy(
                    src_ref=src.at[s, :, columns],
                    dst_ref=dst.at[s, mine, :],
                    send_sem=send_sem.at[s, a],
                    recv_sem=recv_sem.at[s, a],
                    device_id=p,
                    device_id_type=MESH,
                ).start()

    def wait_slabs(s, sem):
        for a, (src, dst) in enumerate(arrays):
            all_but_one = dst.at[s, pl.ds(0, len(peers) * rows), :]
            pltpu.make_async_copy(all_but_one, all_but_one, sem.at[s, a]).wait()

    def correlate(s):
        for i in range(NBLK):
            lo = BLK * i
            product = nt(o_slab[s, lo : lo + BLK, :], w_slab[s, lo:, :]) + nt(w_slab[s, lo : lo + BLK, :], o_slab[s, lo:, :])
            for j in range(i, NBLK):
                at = (FIRST[i] + j - i) * BLK
                part[s, at : at + BLK, :] = product[:, (j - i) * BLK : (j - i + 1) * BLK] * (-0.5 / NG)

    def span(start, size):
        return pl.ds(pl.multiple_of(start, 8), size)

    def total(s, between):
        used = []

        def stage(t, transfers):
            copies = []
            for src, dst, to in transfers:
                at = len(used) + len(copies)
                copies.append(
                    pltpu.make_async_remote_copy(
                        src_ref=src, dst_ref=dst, send_sem=out_sem.at[s, at], recv_sem=in_sem.at[s, at], device_id=to, device_id_type=MESH
                    )
                )
            for copy in copies:
                copy.start()
            between(t)
            for copy in copies:
                copy.wait_recv()
            used.extend(copies)

        stage(0, [(part.at[s, span((1 - core) * HALF, HALF), :], half.at[s], partner)])
        half[s] = half[s] + part[s, span(core * HALF, HALF), :]
        side = HALF // 2
        xs = [ahead(x, k, XS) for k in range(1, XS)]
        ys = [ahead(y, k, YS) for k in range(1, YS)]
        zs = [ahead(z, k, ZS) for k in range(1, ZS)]
        stage(
            1,
            [(half.at[s, span(xx * PART, PART), :], from_x.at[s, k], device(xx, y, z, core)) for k, xx in enumerate(xs)]
            + [(half.at[s, span(side + yy * PART, PART), :], from_y.at[s, k], device(x, yy, z, core)) for k, yy in enumerate(ys)],
        )
        third[s, :PART, :] = half[s, span(x * PART, PART), :] + (from_x[s, 0] + from_x[s, 1] + from_x[s, 2])
        third[s, PART:, :] = half[s, span(side + y * PART, PART), :] + (from_y[s, 0] + from_y[s, 1] + from_y[s, 2])
        stage(2, [(third.at[s, span(zz * CHUNK, CHUNK), :], from_z.at[s, k], device(x, y, zz, core)) for k, zz in enumerate(zs)])
        got = [from_z[s, k] for k in range(ZS - 1)]
        fourth[s] = third[s, span(z * CHUNK, CHUNK), :] + (
            ((got[0] + got[1]) + (got[2] + got[3])) + ((got[4] + got[5]) + got[6])
        )
        upper = z // (ZS // 2)
        stage(
            3,
            [
                (fourth.at[s], from_4.at[s, k - 1], device(ahead(x, k * upper, XS), ahead(y, k * (1 - upper), YS), z, core))
                for k in range(1, 4)
            ],
        )
        start_x = core * HALF + x * PART
        start_y = core * HALF + side + y * PART
        start = (1 - upper) * (start_x + z * CHUNK) + upper * (start_y + (z - ZS // 2) * CHUNK)
        g_out[s, span(start, CHUNK), :] = fourth[s] + (from_4[s, 0] + from_4[s, 1] + from_4[s, 2])
        here = g_out.at[s, span(start, CHUNK), :]
        stage(4, [(here, here, device(x, y, zz, core)) for zz in zs])
        along_x = g_out.at[s, span(start_x, PART), :]
        along_y = g_out.at[s, span(start_y, PART), :]
        stage(
            5,
            [(along_x, along_x, device(xx, y, z, core)) for xx in xs] + [(along_y, along_y, device(x, yy, z, core)) for yy in ys],
        )
        share = g_out.at[s, span(core * HALF, HALF), :]
        stage(6, [(share, share, partner)])
        return used

    cuts = [0, 12, 16, 20, 24, 28, 31, 31, 31]
    batches = [peers[i:j] for i, j in zip(cuts, cuts[1:])]
    send_slabs(0, peers)
    send_slabs(1, batches[0])
    for copy in local:
        copy.wait()
    wait_slabs(0, recv_sem)
    keep = [pltpu.make_async_copy(w_slab.at[s], w_out.at[s], keep_sem.at[s]) for s in range(SETS)]
    keep[0].start()
    correlate(0)
    used = total(0, lambda t: send_slabs(1, batches[t + 1]))
    wait_slabs(1, recv_sem)
    keep[1].start()
    correlate(1)
    used = used + total(1, lambda t: None)
    for copy in used:
        copy.wait_send()
    for copy in keep:
        copy.wait()
    for s in range(SETS):
        wait_slabs(s, send_sem)


def finish_kernel(g_ref, w_ref, out_ref, g, x, a, m, u, slab, result, in_sem, out_sem):
    fetch = pltpu.make_async_copy(w_ref, slab, in_sem)
    fetch.start()
    g[...] = g_ref[...]
    factor(g, x, a, m, u)
    fetch.wait()
    stores = []
    for s in range(SETS):
        for i in range(NBLK):
            lo, hi = BLK * i, BLK * i + BLK
            inverse = x[s, lo:hi, :hi]
            head = inverse.astype(BF16)
            tail = (inverse - head.astype(F32)).astype(BF16)
            known = slab[s, :hi, :]
            result[s, lo:hi, :] = jnp.dot(head, known, preferred_element_type=F32) + jnp.dot(
                tail, known, preferred_element_type=F32
            )
            here = result.at[s, pl.ds(lo, BLK), :]
            stores.append(pltpu.make_async_copy(here, out_ref.at[s, pl.ds(lo, BLK), :], out_sem.at[s, i]))
            stores[-1].start()
    for store in stores:
        store.wait()


def per_device(orbitals, exchange_applied):
    width = orbitals.shape[2] // (YS * ZS)
    vmem = pl.BlockSpec(memory_space=pltpu.VMEM)
    anywhere = pl.BlockSpec(memory_space=pl.ANY)
    gram, slab = pl.pallas_call(
        exchange_kernel,
        out_shape=(
            jax.ShapeDtypeStruct((SETS, GROWS, BLK), F32),
            jax.ShapeDtypeStruct((SETS, NB, width), BF16),
        ),
        in_specs=[anywhere, anywhere],
        out_specs=(vmem, anywhere),
        scratch_shapes=[
            pltpu.VMEM((SETS, NB, width), BF16),
            pltpu.VMEM((SETS, NB, width), BF16),
            pltpu.VMEM((SETS, GROWS, BLK), F32),
            pltpu.VMEM((SETS, HALF, BLK), F32),
            pltpu.VMEM((SETS, XS - 1, PART, BLK), F32),
            pltpu.VMEM((SETS, YS - 1, PART, BLK), F32),
            pltpu.VMEM((SETS, 2 * PART, BLK), F32),
            pltpu.VMEM((SETS, ZS - 1, CHUNK, BLK), F32),
            pltpu.VMEM((SETS, CHUNK, BLK), F32),
            pltpu.VMEM((SETS, 3, CHUNK, BLK), F32),
            pltpu.SemaphoreType.DMA((SETS, 2)),
            pltpu.SemaphoreType.DMA((SETS, 2)),
            pltpu.SemaphoreType.DMA((SETS, 2)),
            pltpu.SemaphoreType.DMA((SETS, 31)),
            pltpu.SemaphoreType.DMA((SETS, 31)),
            pltpu.SemaphoreType.DMA((SETS,)),
        ],
        compiler_params=pltpu.CompilerParams(collective_id=0, has_side_effects=True, vmem_limit_bytes=VMEM_LIMIT),
    )(orbitals, exchange_applied)
    return pl.pallas_call(
        finish_kernel,
        out_shape=jax.ShapeDtypeStruct((SETS, NB, width), F32),
        in_specs=[vmem, anywhere],
        out_specs=anywhere,
        scratch_shapes=[
            pltpu.VMEM((SETS, GROWS, BLK), F32),
            pltpu.VMEM((SETS, NB, NB), F32),
            pltpu.VMEM((BLK, 2 * BLK), F32),
            pltpu.VMEM((BLK, 2 * BLK), F32),
            pltpu.VMEM((SETS, BLK, NB), F32),
            pltpu.VMEM((SETS, NB, width), BF16),
            pltpu.VMEM((SETS, NB, width), F32),
            pltpu.SemaphoreType.DMA,
            pltpu.SemaphoreType.DMA((SETS, NBLK)),
        ],
        compiler_params=pltpu.CompilerParams(vmem_limit_bytes=VMEM_LIMIT),
    )(gram, slab)


def solution(mesh):
    placed = (P(None, "ga", "ba"), P(None, "ga", "ba"))
    return jax.shard_map(
        per_device,
        mesh=mesh,
        in_specs=placed,
        out_specs=P(None, None, ("ba", "ga")),
        check_vma=False,
    )
```

```python
import functools

import jax
import jax.numpy as jnp
from jax import lax
from jax.experimental import pallas as pl
from jax.experimental.pallas import tpu as pltpu
from jax.sharding import PartitionSpec as P

MESH = pl.DeviceIdType.MESH
F32 = jnp.float32
BF16 = jnp.bfloat16
NB, NG, SETS = 512, 294912, 2
BLK = 128
HB = BLK // 2
NBLK = NB // BLK
PANEL = 16
PAIRS = [(i, j) for i in range(NBLK) for j in range(i, NBLK)]
FIRST = [PAIRS.index((i, i)) for i in range(NBLK)]
USED = len(PAIRS) * BLK
GROWS = 12 * BLK
LROWS = 16 * BLK
XS, YS, ZS = 4, 4, 8
HALF = GROWS // 2
PLANES = XS * YS
CHUNK = HALF // (PLANES + ZS)
PARTA = CHUNK * ZS
LHALF = LROWS // 2
LPLANE = LHALF // PLANES
LCHUNK = LPLANE // ZS
MESSAGES = 2 + 3 * (PLANES - 1 + ZS - 1)
VMEM_LIMIT = 60 * 2**20

def ring(d, n):
    return min(d, n - d)


OFFSETS = sorted(
    [(dy, dz) for dy in range(YS) for dz in range(ZS) if (dy, dz) != (0, 0)],
    key=lambda t: ring(t[0], YS) + ring(t[1], ZS),
)


PLANE = sorted(
    [(dy, dx) for dy in range(YS) for dx in range(XS) if (dy, dx) != (0, 0)],
    key=lambda t: -ring(t[0], YS) - ring(t[1], XS),
)


def pieces(a):
    head = a.astype(BF16)
    rest = a - head.astype(F32)
    middle = rest.astype(BF16)
    return head, middle, (rest - middle.astype(F32)).astype(BF16)


def stacked(left, right, axis_left, axis_right):
    a, b = pieces(left), pieces(right)
    order = ((0, 0), (0, 1), (1, 0), (1, 1), (0, 2), (2, 0))
    return lax.dot_general(
        jnp.concatenate([a[i] for i, _ in order], axis=axis_left),
        jnp.concatenate([b[j] for _, j in order], axis=axis_right),
        (((axis_left,), (axis_right,)), ((), ())),
        preferred_element_type=F32,
    )


def tn(a, b):
    return stacked(a, b, 0, 0)


def nn(a, b):
    return stacked(a, b, 1, 0)


def nt(a, b):
    return lax.dot_general(a, b, (((1,), (1,)), ((), ())), preferred_element_type=F32)


def pack(first, second):
    return jnp.concatenate([first[:, :HB], second[:, :HB], first[:, HB:], second[:, HB:]], axis=1)


def unpack(packed):
    return (
        jnp.concatenate([packed[:, :HB], packed[:, BLK : BLK + HB]], axis=1),
        jnp.concatenate([packed[:, HB:BLK], packed[:, BLK + HB :]], axis=1),
    )


def factor_blocks(a_ref, x_ref):
    wide = (8, BLK)
    sub = lax.broadcasted_iota(jnp.int32, wide, 0)
    left = lax.broadcasted_iota(jnp.int32, wide, 1) < HB
    rows = lax.broadcasted_iota(jnp.int32, (BLK, 2 * BLK), 0)
    cols = lax.broadcasted_iota(jnp.int32, (BLK, 2 * BLK), 1)
    x_ref[...] = jnp.where(rows == cols % HB + cols // BLK * HB, 1.0, 0.0).astype(F32)
    own = PANEL // 8
    for base in range(0, BLK, PANEL):
        v = own if base + PANEL == BLK else 2 * own
        at = [slice(base + 8 * i, base + 8 * i + 8) for i in range(v)]
        t = [[a_ref[at[i], :BLK], a_ref[at[i], BLK:], x_ref[at[i], :BLK], x_ref[at[i], BLK:]] for i in range(v)]
        side, first = divmod(base, HB)
        c = [
            [
                jnp.where(
                    left,
                    jnp.broadcast_to(t[i][side][:, first + r : first + r + 1], wide),
                    jnp.broadcast_to(t[i][side][:, HB + first + r : HB + first + r + 1], wide),
                )
                for i in range(v)
            ]
            for r in range(PANEL)
        ]
        live = [k for k in range(4) if not (k == 0 and side == 1) and not (k == 3 and side == 0 and base + 2 * PANEL <= HB)]
        d = [jnp.ones(wide, F32) for _ in range(own)]
        for r in range(PANEL):
            h, q = divmod(r, 8)
            pivot = jnp.broadcast_to(c[r][h][q : q + 1, :], wide)
            inv = 1.0 / pivot
            d[h] = jnp.where(sub == q, pivot, d[h])
            trow = {k: jnp.broadcast_to(t[h][k][q : q + 1, :], wide) for k in live}
            crow = {j: jnp.broadcast_to(c[j][h][q : q + 1, :], wide) for j in range(r + 1, PANEL)}
            for i in range(h, v):
                if i == h and q == 7:
                    continue
                m = c[r][i] * inv
                if i == h:
                    m = jnp.where(sub > q, m, 0.0)
                for j in range(r + 1, PANEL):
                    c[j][i] = c[j][i] - m * crow[j]
                for k in live:
                    t[i][k] = t[i][k] - m * trow[k]
        for i in range(own):
            s = lax.rsqrt(d[i])
            t[i] = [e * s for e in t[i]]
        for i in range(v):
            a_ref[at[i], :BLK], a_ref[at[i], BLK:], x_ref[at[i], :BLK], x_ref[at[i], BLK:] = t[i]
        rest = base + 2 * PANEL
        if rest < BLK:
            u = a_ref[base : base + PANEL, :]
            w = x_ref[base : base + PANEL, :]
            both = jnp.concatenate([u, w], axis=1)
            for lo in (0, HB):
                if rest >= lo + HB:
                    continue
                skip = max(rest - lo, 0)
                p = tn(u[:, 2 * lo : 2 * lo + BLK], both)
                pick = lax.broadcasted_iota(jnp.int32, (HB - skip, 4 * BLK), 1) % BLK < HB
                update = jnp.where(pick, p[skip:HB], p[HB + skip :])
                if lo == 0 or rest <= HB:
                    a_ref[lo + skip : lo + HB, :] = a_ref[lo + skip : lo + HB, :] - update[:, : 2 * BLK]
                else:
                    a_ref[lo + skip : lo + HB, BLK:] = a_ref[lo + skip : lo + HB, BLK:] - update[:, BLK : 2 * BLK]
                x_ref[lo + skip : lo + HB, :] = x_ref[lo + skip : lo + HB, :] - update[:, 2 * BLK :]


def factor(g_ref, x_ref, a_ref, m_ref, u_ref):
    def block(i, j):
        at = (FIRST[i] + j - i) * BLK
        return slice(at, at + BLK)

    x_ref[...] = jnp.zeros((SETS, NB, NB), F32)

    def step(k, carry):
        diagonal = pl.ds(pl.multiple_of(k * (2 * NBLK + 1 - k) // 2 * BLK, BLK), BLK)
        a_ref[...] = pack(g_ref[0, diagonal, :], g_ref[1, diagonal, :])
        factor_blocks(a_ref, m_ref)
        ms = unpack(m_ref[...])
        for kk in range(NBLK):
            @pl.when(k == kk)
            def _():
                lo, hi = BLK * kk, BLK * kk + BLK
                for s, m in enumerate(ms):
                    if kk:
                        x_ref[s, lo:hi, :lo] = nn(m, x_ref[s, lo:hi, :lo])
                    x_ref[s, lo:hi, lo:hi] = m
                    for j in range(kk + 1, NBLK):
                        u_ref[s, :, j * BLK : (j + 1) * BLK] = nn(m, g_ref[s, block(kk, j), :])
                for s, m in enumerate(ms):
                    for i in range(kk + 1, NBLK):
                        li = BLK * i
                        ui = u_ref[s, :, li : li + BLK]
                        update = tn(ui, u_ref[s, :, li:])
                        for j in range(i, NBLK):
                            g_ref[s, block(i, j), :] = g_ref[s, block(i, j), :] - update[:, (j - i) * BLK : (j - i + 1) * BLK]
                        x_ref[s, li : li + BLK, :hi] = x_ref[s, li : li + BLK, :hi] - tn(ui, x_ref[s, lo:hi, :hi])
        return carry

    lax.fori_loop(0, NBLK, step, 0)


def exchange_kernel(
    o_ref, w_ref, g_out, w_out, o_slab, w_slab, part, g_sum, half, once, from_a, from_b, then_a, then_b, light, middle, from_p, from_q,
    send_sem, recv_sem, own_sem, out_sem, in_sem, keep_sem, gram_sem
):
    ga, ba = lax.axis_index("ga"), lax.axis_index("ba")
    y, z = ga // ZS, lax.rem(ga, ZS)
    x, core = ba // 2, lax.rem(ba, 2)

    def device(x, y, z, core):
        return (y * ZS + z, x * 2 + core)

    def ahead(i, k, n):
        return lax.rem(i + k, n)

    def span(start, size):
        return pl.ds(pl.multiple_of(start, 8), size)

    peers = [device(x, ahead(y, dy, YS), ahead(z, dz, ZS), core) for dy, dz in OFFSETS]
    partner = device(x, y, z, 1 - core)
    line = [(k, device(x, y, ahead(z, k, ZS), core), ahead(z, k, ZS)) for k in range(1, ZS)]
    plane = [
        (dy * XS + dx, device(ahead(x, dx, XS), ahead(y, dy, YS), z, core), ahead(y, dy, YS) * XS + ahead(x, dx, XS))
        for dy, dx in PLANE
    ]
    spot = y * XS + x
    greeted = [*peers, partner, *(to for (dy, dx), (_, to, _) in zip(PLANE, plane) if dx)]
    barrier = pltpu.get_barrier_semaphore()
    for p in greeted:
        pl.semaphore_signal(barrier, inc=1, device_id=p, device_id_type=MESH)
    width = o_slab.shape[2]
    rows = o_ref.shape[1]
    mine = pl.ds(pl.multiple_of(ga * rows, rows), rows)
    own = pl.ds(pl.multiple_of(ga * width, BLK), width)
    arrays = ((o_ref, o_slab), (w_ref, w_slab))
    local = [
        pltpu.make_async_copy(src.at[s, :, own], dst.at[s, mine, :], own_sem.at[s, a])
        for s in range(SETS)
        for a, (src, dst) in enumerate(arrays)
    ]
    for copy in local:
        copy.start()
    part[:, USED:, :] = jnp.zeros((SETS, LROWS - USED, BLK), F32)
    pl.semaphore_wait(barrier, len(greeted))

    def send_slabs(s, chosen):
        for p in chosen:
            columns = pl.ds(pl.multiple_of(p[0] * width, BLK), width)
            for a, (src, dst) in enumerate(arrays):
                pltpu.make_async_remote_copy(
                    src_ref=src.at[s, :, columns],
                    dst_ref=dst.at[s, mine, :],
                    send_sem=send_sem.at[s, a],
                    recv_sem=recv_sem.at[s, a],
                    device_id=p,
                    device_id_type=MESH,
                ).start()

    def wait_slabs(s, sem):
        for a, (src, dst) in enumerate(arrays):
            all_but_one = dst.at[s, pl.ds(0, len(peers) * rows), :]
            pltpu.make_async_copy(all_but_one, all_but_one, sem.at[s, a]).wait()

    def correlate(s):
        for i in range(NBLK):
            lo = BLK * i
            product = nt(o_slab[s, lo : lo + BLK, :], w_slab[s, lo:, :]) + nt(w_slab[s, lo : lo + BLK, :], o_slab[s, lo:, :])
            for j in range(i, NBLK):
                at = (FIRST[i] + j - i) * BLK
                part[s, at : at + BLK, :] = product[:, (j - i) * BLK : (j - i + 1) * BLK] * (-0.5 / NG)

    used = [[], []]

    def stage(s, transfers, between=None):
        copies = [
            pltpu.make_async_remote_copy(
                src_ref=src, dst_ref=dst, send_sem=out_sem.at[s, at], recv_sem=in_sem.at[s, at], device_id=to, device_id_type=MESH
            )
            for at, (src, dst, to) in enumerate(transfers, len(used[s]))
        ]
        for copy in copies:
            copy.start()
        if between is not None:
            send_slabs(1, between)
        for copy in copies:
            copy.wait_recv()
        used[s].extend(copies)

    def added(terms):
        while len(terms) > 1:
            terms = [sum(terms[i : i + 2][1:], terms[i]) for i in range(0, len(terms), 2)]
        return terms[0]

    def total_light(s, batches):
        stage(s, [(part.at[s, span((1 - core) * LHALF, LHALF), :], light, partner)], batches[0])
        light[...] = light[...] + part[s, span(core * LHALF, LHALF), :]
        stage(s, [(light.at[span(i * LPLANE, LPLANE), :], from_p.at[k], to) for k, to, i in plane], batches[1])
        middle[...] = added([light[span(spot * LPLANE, LPLANE), :]] + [from_p[k] for k in range(1, PLANES)])
        stage(s, [(middle.at[span(i * LCHUNK, LCHUNK), :], from_q.at[k], to) for k, to, i in line], batches[2])
        start = core * LHALF + spot * LPLANE
        here = span(start + z * LCHUNK, LCHUNK)
        g_sum[s, here, :] = added([middle[span(z * LCHUNK, LCHUNK), :]] + [from_q[k] for k in range(1, ZS)])
        for batch, done, to_all in (
            (batches[3], g_sum.at[s, here, :], [to for _, to, _ in line]),
            (batches[4], g_sum.at[s, span(start, LPLANE), :], [to for _, to, _ in plane]),
            (batches[5], g_sum.at[s, span(core * LHALF, LHALF), :], [partner]),
        ):
            stage(s, [(done, done, to) for to in to_all], batch)

    def total(s):
        stage(s, [(part.at[s, span((1 - core) * HALF, HALF), :], half, partner)])
        half[...] = half[...] + part[s, span(core * HALF, HALF), :]
        stage(
            s,
            [(half.at[span(PARTA + i * CHUNK, CHUNK), :], from_b.at[k], to) for k, to, i in plane]
            + [(half.at[span(i * CHUNK, CHUNK), :], from_a.at[k], to) for k, to, i in line],
        )
        once[0] = added([half[span(z * CHUNK, CHUNK), :]] + [from_a[k] for k in range(1, ZS)])
        once[1] = added([half[span(PARTA + spot * CHUNK, CHUNK), :]] + [from_b[k] for k in range(1, PLANES)])
        stage(s, [(once.at[0], then_a.at[k], to) for k, to, _ in plane] + [(once.at[1], then_b.at[k], to) for k, to, _ in line])
        start_a = span(core * HALF + z * CHUNK, CHUNK)
        start_b = span(core * HALF + PARTA + spot * CHUNK, CHUNK)
        g_sum[s, start_a, :] = added([once[0]] + [then_a[k] for k in range(1, PLANES)])
        g_sum[s, start_b, :] = added([once[1]] + [then_b[k] for k in range(1, ZS)])
        here_a, here_b = g_sum.at[s, start_a, :], g_sum.at[s, start_b, :]
        stage(s, [(here_b, here_b, to) for _, to, _ in plane] + [(here_a, here_a, to) for _, to, _ in line])
        share = g_sum.at[s, span(core * HALF, HALF), :]
        stage(s, [(share, share, partner)])

    cuts = [0, 12, 16, 20, 24, 28, 31, 31]
    batches = [peers[i:j] for i, j in zip(cuts, cuts[1:])]
    send_slabs(0, peers)
    send_slabs(1, batches[0])
    for copy in local:
        copy.wait()
    wait_slabs(0, recv_sem)
    keep = [pltpu.make_async_copy(w_slab.at[s], w_out.at[s], keep_sem.at[s]) for s in range(SETS)]
    keep_gram = [pltpu.make_async_copy(g_sum.at[s, pl.ds(0, USED), :], g_out.at[s], gram_sem.at[s]) for s in range(SETS)]
    keep[0].start()
    correlate(0)
    total_light(0, batches[1:])
    keep_gram[0].start()
    wait_slabs(1, recv_sem)
    keep[1].start()
    correlate(1)
    total(1)
    keep_gram[1].start()
    for copy in used[0] + used[1]:
        copy.wait_send()
    for s in range(SETS):
        wait_slabs(s, send_sem)
    for copy in keep + keep_gram:
        copy.wait()


def finish_kernel(g_ref, w_ref, out_ref, g, x, a, m, u, slab, result, in_sem, out_sem):
    fetch = pltpu.make_async_copy(w_ref, slab, in_sem)
    fetch.start()
    g[...] = g_ref[...]
    factor(g, x, a, m, u)
    fetch.wait()
    stores = []
    for s in range(SETS):
        for i in range(NBLK):
            lo, hi = BLK * i, BLK * i + BLK
            inverse = x[s, lo:hi, :hi]
            head = inverse.astype(BF16)
            tail = (inverse - head.astype(F32)).astype(BF16)
            known = slab[s, :hi, :]
            result[s, lo:hi, :] = jnp.dot(head, known, preferred_element_type=F32) + jnp.dot(
                tail, known, preferred_element_type=F32
            )
            here = result.at[s, pl.ds(lo, BLK), :]
            stores.append(pltpu.make_async_copy(here, out_ref.at[s, pl.ds(lo, BLK), :], out_sem.at[s, i]))
            stores[-1].start()
    for store in stores:
        store.wait()


def per_device(orbitals, exchange_applied):
    width = orbitals.shape[2] // (YS * ZS)
    vmem = pl.BlockSpec(memory_space=pltpu.VMEM)
    anywhere = pl.BlockSpec(memory_space=pl.ANY)
    gram, slab = pl.pallas_call(
        exchange_kernel,
        out_shape=(
            jax.ShapeDtypeStruct((SETS, USED, BLK), F32),
            jax.ShapeDtypeStruct((SETS, NB, width), BF16),
        ),
        in_specs=[anywhere, anywhere],
        out_specs=(anywhere, anywhere),
        scratch_shapes=[
            pltpu.VMEM((SETS, NB, width), BF16),
            pltpu.VMEM((SETS, NB, width), BF16),
            pltpu.VMEM((SETS, LROWS, BLK), F32),
            pltpu.VMEM((SETS, LROWS, BLK), F32),
            pltpu.VMEM((HALF, BLK), F32),
            pltpu.VMEM((2, CHUNK, BLK), F32),
            pltpu.VMEM((ZS, CHUNK, BLK), F32),
            pltpu.VMEM((PLANES, CHUNK, BLK), F32),
            pltpu.VMEM((PLANES, CHUNK, BLK), F32),
            pltpu.VMEM((ZS, CHUNK, BLK), F32),
            pltpu.VMEM((LHALF, BLK), F32),
            pltpu.VMEM((LPLANE, BLK), F32),
            pltpu.VMEM((PLANES, LPLANE, BLK), F32),
            pltpu.VMEM((ZS, LCHUNK, BLK), F32),
            pltpu.SemaphoreType.DMA((SETS, 2)),
            pltpu.SemaphoreType.DMA((SETS, 2)),
            pltpu.SemaphoreType.DMA((SETS, 2)),
            pltpu.SemaphoreType.DMA((SETS, MESSAGES)),
            pltpu.SemaphoreType.DMA((SETS, MESSAGES)),
            pltpu.SemaphoreType.DMA((SETS,)),
            pltpu.SemaphoreType.DMA((SETS,)),
        ],
        compiler_params=pltpu.CompilerParams(collective_id=0, has_side_effects=True, vmem_limit_bytes=VMEM_LIMIT),
    )(orbitals, exchange_applied)
    return pl.pallas_call(
        finish_kernel,
        out_shape=jax.ShapeDtypeStruct((SETS, NB, width), F32),
        in_specs=[vmem, anywhere],
        out_specs=anywhere,
        scratch_shapes=[
            pltpu.VMEM((SETS, USED, BLK), F32),
            pltpu.VMEM((SETS, NB, NB), F32),
            pltpu.VMEM((BLK, 2 * BLK), F32),
            pltpu.VMEM((BLK, 2 * BLK), F32),
            pltpu.VMEM((SETS, BLK, NB), F32),
            pltpu.VMEM((SETS, NB, width), BF16),
            pltpu.VMEM((SETS, NB, width), F32),
            pltpu.SemaphoreType.DMA,
            pltpu.SemaphoreType.DMA((SETS, NBLK)),
        ],
        compiler_params=pltpu.CompilerParams(vmem_limit_bytes=VMEM_LIMIT),
    )(gram, slab)


def solution(mesh):
    placed = (P(None, "ga", "ba"), P(None, "ga", "ba"))
    return jax.shard_map(
        per_device,
        mesh=mesh,
        in_specs=placed,
        out_specs=P(None, None, ("ba", "ga")),
        check_vma=False,
    )
```

```python
import functools

import jax
import jax.numpy as jnp
from jax import lax
from jax.experimental import pallas as pl
from jax.experimental.pallas import tpu as pltpu
from jax.sharding import PartitionSpec as P

MESH = pl.DeviceIdType.MESH
F32 = jnp.float32
BF16 = jnp.bfloat16
NB, NG, SETS = 512, 294912, 2
BLK = 128
HB = BLK // 2
NBLK = NB // BLK
PANEL = 16
PAIRS = [(i, j) for i in range(NBLK) for j in range(i, NBLK)]
FIRST = [PAIRS.index((i, i)) for i in range(NBLK)]
USED = len(PAIRS) * BLK
GROWS = 12 * BLK
LROWS = 16 * BLK
XS, YS, ZS = 4, 4, 8
HALF = GROWS // 2
PLANES = XS * YS
CHUNK = HALF // (PLANES + ZS)
PARTA = CHUNK * ZS
LHALF = LROWS // 2
LPLANE = LHALF // PLANES
LCHUNK = LPLANE // ZS
MESSAGES = 2 + 3 * (PLANES - 1 + ZS - 1)
VMEM_LIMIT = 50 * 2**20

def ring(d, n):
    return min(d, n - d)


OFFSETS = sorted(
    [(dy, dz) for dy in range(YS) for dz in range(ZS) if (dy, dz) != (0, 0)],
    key=lambda t: ring(t[0], YS) + ring(t[1], ZS),
)


PLANE = sorted(
    [(dy, dx) for dy in range(YS) for dx in range(XS) if (dy, dx) != (0, 0)],
    key=lambda t: -ring(t[0], YS) - ring(t[1], XS),
)


def pieces(a):
    head = a.astype(BF16)
    rest = a - head.astype(F32)
    middle = rest.astype(BF16)
    return head, middle, (rest - middle.astype(F32)).astype(BF16)


def stacked(left, right, axis_left, axis_right):
    a, b = pieces(left), pieces(right)
    order = ((0, 0), (0, 1), (1, 0), (1, 1), (0, 2), (2, 0))
    return lax.dot_general(
        jnp.concatenate([a[i] for i, _ in order], axis=axis_left),
        jnp.concatenate([b[j] for _, j in order], axis=axis_right),
        (((axis_left,), (axis_right,)), ((), ())),
        preferred_element_type=F32,
    )


def tn(a, b):
    return stacked(a, b, 0, 0)


def nn(a, b):
    return stacked(a, b, 1, 0)


def nt(a, b):
    return lax.dot_general(a, b, (((1,), (1,)), ((), ())), preferred_element_type=F32)


def pack(first, second):
    return jnp.concatenate([first[:, :HB], second[:, :HB], first[:, HB:], second[:, HB:]], axis=1)


def unpack(packed):
    return (
        jnp.concatenate([packed[:, :HB], packed[:, BLK : BLK + HB]], axis=1),
        jnp.concatenate([packed[:, HB:BLK], packed[:, BLK + HB :]], axis=1),
    )


def factor_blocks(a_ref, x_ref):
    wide = (8, BLK)
    sub = lax.broadcasted_iota(jnp.int32, wide, 0)
    left = lax.broadcasted_iota(jnp.int32, wide, 1) < HB
    rows = lax.broadcasted_iota(jnp.int32, (BLK, 2 * BLK), 0)
    cols = lax.broadcasted_iota(jnp.int32, (BLK, 2 * BLK), 1)
    x_ref[...] = jnp.where(rows == cols % HB + cols // BLK * HB, 1.0, 0.0).astype(F32)
    own = PANEL // 8
    for base in range(0, BLK, PANEL):
        v = own if base + PANEL == BLK else 2 * own
        at = [slice(base + 8 * i, base + 8 * i + 8) for i in range(v)]
        t = [[a_ref[at[i], :BLK], a_ref[at[i], BLK:], x_ref[at[i], :BLK], x_ref[at[i], BLK:]] for i in range(v)]
        side, first = divmod(base, HB)
        c = [
            [
                jnp.where(
                    left,
                    jnp.broadcast_to(t[i][side][:, first + r : first + r + 1], wide),
                    jnp.broadcast_to(t[i][side][:, HB + first + r : HB + first + r + 1], wide),
                )
                for i in range(v)
            ]
            for r in range(PANEL)
        ]
        live = [k for k in range(4) if not (k == 0 and side == 1) and not (k == 3 and side == 0 and base + 2 * PANEL <= HB)]
        d = [jnp.ones(wide, F32) for _ in range(own)]
        for r in range(PANEL):
            h, q = divmod(r, 8)
            pivot = jnp.broadcast_to(c[r][h][q : q + 1, :], wide)
            inv = 1.0 / pivot
            d[h] = jnp.where(sub == q, pivot, d[h])
            trow = {k: jnp.broadcast_to(t[h][k][q : q + 1, :], wide) for k in live}
            crow = {j: jnp.broadcast_to(c[j][h][q : q + 1, :], wide) for j in range(r + 1, PANEL)}
            for i in range(h, v):
                if i == h and q == 7:
                    continue
                m = c[r][i] * inv
                if i == h:
                    m = jnp.where(sub > q, m, 0.0)
                for j in range(r + 1, PANEL):
                    c[j][i] = c[j][i] - m * crow[j]
                for k in live:
                    t[i][k] = t[i][k] - m * trow[k]
        for i in range(own):
            s = lax.rsqrt(d[i])
            t[i] = [e * s for e in t[i]]
        for i in range(v):
            a_ref[at[i], :BLK], a_ref[at[i], BLK:], x_ref[at[i], :BLK], x_ref[at[i], BLK:] = t[i]
        rest = base + 2 * PANEL
        if rest < BLK:
            u = a_ref[base : base + PANEL, :]
            w = x_ref[base : base + PANEL, :]
            both = jnp.concatenate([u, w], axis=1)
            for lo in (0, HB):
                if rest >= lo + HB:
                    continue
                skip = max(rest - lo, 0)
                p = tn(u[:, 2 * lo : 2 * lo + BLK], both)
                pick = lax.broadcasted_iota(jnp.int32, (HB - skip, 4 * BLK), 1) % BLK < HB
                update = jnp.where(pick, p[skip:HB], p[HB + skip :])
                if lo == 0 or rest <= HB:
                    a_ref[lo + skip : lo + HB, :] = a_ref[lo + skip : lo + HB, :] - update[:, : 2 * BLK]
                else:
                    a_ref[lo + skip : lo + HB, BLK:] = a_ref[lo + skip : lo + HB, BLK:] - update[:, BLK : 2 * BLK]
                x_ref[lo + skip : lo + HB, :] = x_ref[lo + skip : lo + HB, :] - update[:, 2 * BLK :]


def factor(g_ref, x_ref, a_ref, m_ref, u_ref):
    def block(i, j):
        at = (FIRST[i] + j - i) * BLK
        return slice(at, at + BLK)

    x_ref[...] = jnp.zeros((SETS, NB, NB), F32)

    def step(k, carry):
        diagonal = pl.ds(pl.multiple_of(k * (2 * NBLK + 1 - k) // 2 * BLK, BLK), BLK)
        a_ref[...] = pack(g_ref[0, diagonal, :], g_ref[1, diagonal, :])
        factor_blocks(a_ref, m_ref)
        ms = unpack(m_ref[...])
        for kk in range(NBLK):
            @pl.when(k == kk)
            def _():
                lo, hi = BLK * kk, BLK * kk + BLK
                below = NB - hi
                for s, m in enumerate(ms):
                    x_ref[s, lo:hi, lo:hi] = m
                    right = [g_ref[s, block(kk, j), :] for j in range(kk + 1, NBLK)]
                    left = [x_ref[s, lo:hi, :lo]] if kk else []
                    row = nn(m, jnp.concatenate(right + left, axis=1))
                    if below:
                        u_ref[s, :, hi:] = row[:, :below]
                    if kk:
                        x_ref[s, lo:hi, :lo] = row[:, below:]
                if below:
                    for s in range(SETS):
                        u = u_ref[s, :, hi:]
                        update = nn(u.T, jnp.concatenate([u, x_ref[s, lo:hi, :hi]], axis=1))
                        for i in range(kk + 1, NBLK):
                            at = slice(BLK * i - hi, BLK * i - hi + BLK)
                            for j in range(i, NBLK):
                                g_ref[s, block(i, j), :] = g_ref[s, block(i, j), :] - update[at, BLK * j - hi : BLK * j - hi + BLK]
                            li = BLK * i
                            x_ref[s, li : li + BLK, :hi] = x_ref[s, li : li + BLK, :hi] - update[at, below:]
        return carry

    lax.fori_loop(0, NBLK, step, 0)


def exchange_kernel(
    o_ref, w_ref, g_sum, w_out, o_slab, w_slab, part, half, once, from_a, from_b, then_a, then_b, light, middle, from_p, from_q,
    send_sem, recv_sem, own_sem, out_sem, in_sem, keep_sem
):
    ga, ba = lax.axis_index("ga"), lax.axis_index("ba")
    y, z = ga // ZS, lax.rem(ga, ZS)
    x, core = ba // 2, lax.rem(ba, 2)

    def device(x, y, z, core):
        return (y * ZS + z, x * 2 + core)

    def ahead(i, k, n):
        return lax.rem(i + k, n)

    def span(start, size):
        return pl.ds(pl.multiple_of(start, 8), size)

    peers = [device(x, ahead(y, dy, YS), ahead(z, dz, ZS), core) for dy, dz in OFFSETS]
    partner = device(x, y, z, 1 - core)
    line = [(k, device(x, y, ahead(z, k, ZS), core), ahead(z, k, ZS)) for k in range(1, ZS)]
    plane = [
        (dy * XS + dx, device(ahead(x, dx, XS), ahead(y, dy, YS), z, core), ahead(y, dy, YS) * XS + ahead(x, dx, XS))
        for dy, dx in PLANE
    ]
    spot = y * XS + x
    greeted = [*peers, partner, *(to for (dy, dx), (_, to, _) in zip(PLANE, plane) if dx)]
    barrier = pltpu.get_barrier_semaphore()
    for p in greeted:
        pl.semaphore_signal(barrier, inc=1, device_id=p, device_id_type=MESH)
    width = o_slab.shape[2]
    rows = o_ref.shape[1]
    mine = pl.ds(pl.multiple_of(ga * rows, rows), rows)
    own = pl.ds(pl.multiple_of(ga * width, BLK), width)
    arrays = ((o_ref, o_slab), (w_ref, w_slab))
    local = [
        pltpu.make_async_copy(src.at[s, :, own], dst.at[s, mine, :], own_sem.at[s, a])
        for s in range(SETS)
        for a, (src, dst) in enumerate(arrays)
    ]
    for copy in local:
        copy.start()
    part[:, USED:, :] = jnp.zeros((SETS, LROWS - USED, BLK), F32)
    pl.semaphore_wait(barrier, len(greeted))

    def send_slabs(s, chosen):
        for p in chosen:
            columns = pl.ds(pl.multiple_of(p[0] * width, BLK), width)
            for a, (src, dst) in enumerate(arrays):
                pltpu.make_async_remote_copy(
                    src_ref=src.at[s, :, columns],
                    dst_ref=dst.at[s, mine, :],
                    send_sem=send_sem.at[s, a],
                    recv_sem=recv_sem.at[s, a],
                    device_id=p,
                    device_id_type=MESH,
                ).start()

    def wait_slabs(s, sem):
        for a, (src, dst) in enumerate(arrays):
            all_but_one = dst.at[s, pl.ds(0, len(peers) * rows), :]
            pltpu.make_async_copy(all_but_one, all_but_one, sem.at[s, a]).wait()

    def correlate(s):
        for i in range(0, NBLK, 2):
            lo, hi = BLK * i, BLK * (i + 2)
            product = nt(o_slab[s, lo:hi, :], w_slab[s, lo:, :]) + nt(w_slab[s, lo:hi, :], o_slab[s, lo:, :])
            for k in range(i, i + 2):
                for j in range(k, NBLK):
                    at = (FIRST[k] + j - k) * BLK
                    block = product[(k - i) * BLK : (k - i + 1) * BLK, (j - i) * BLK : (j - i + 1) * BLK]
                    part[s, at : at + BLK, :] = block * (-0.5 / NG)

    used = [[], []]

    def stage(s, transfers, between=None):
        copies = [
            pltpu.make_async_remote_copy(
                src_ref=src, dst_ref=dst, send_sem=out_sem.at[s, at], recv_sem=in_sem.at[s, at], device_id=to, device_id_type=MESH
            )
            for at, (src, dst, to) in enumerate(transfers, len(used[s]))
        ]
        for copy in copies:
            copy.start()
        if between is not None:
            send_slabs(1, between)
        for copy in copies:
            copy.wait_recv()
        used[s].extend(copies)

    def added(terms):
        while len(terms) > 1:
            terms = [sum(terms[i : i + 2][1:], terms[i]) for i in range(0, len(terms), 2)]
        return terms[0]

    def total_light(s, batches):
        stage(s, [(part.at[s, span((1 - core) * LHALF, LHALF), :], light, partner)], batches[0])
        light[...] = light[...] + part[s, span(core * LHALF, LHALF), :]
        stage(s, [(light.at[span(i * LPLANE, LPLANE), :], from_p.at[k], to) for k, to, i in plane], batches[1])
        middle[...] = added([light[span(spot * LPLANE, LPLANE), :]] + [from_p[k] for k in range(1, PLANES)])
        stage(s, [(middle.at[span(i * LCHUNK, LCHUNK), :], from_q.at[k], to) for k, to, i in line], batches[2])
        start = core * LHALF + spot * LPLANE
        here = span(start + z * LCHUNK, LCHUNK)
        g_sum[s, here, :] = added([middle[span(z * LCHUNK, LCHUNK), :]] + [from_q[k] for k in range(1, ZS)])
        for batch, done, to_all in (
            (batches[3], g_sum.at[s, here, :], [to for _, to, _ in line]),
            (batches[4], g_sum.at[s, span(start, LPLANE), :], [to for _, to, _ in plane]),
            (batches[5], g_sum.at[s, span(core * LHALF, LHALF), :], [partner]),
        ):
            stage(s, [(done, done, to) for to in to_all], batch)

    def total(s):
        stage(s, [(part.at[s, span((1 - core) * HALF, HALF), :], half, partner)])
        half[...] = half[...] + part[s, span(core * HALF, HALF), :]
        stage(
            s,
            [(half.at[span(PARTA + i * CHUNK, CHUNK), :], from_b.at[k], to) for k, to, i in plane]
            + [(half.at[span(i * CHUNK, CHUNK), :], from_a.at[k], to) for k, to, i in line],
        )
        once[0] = added([half[span(z * CHUNK, CHUNK), :]] + [from_a[k] for k in range(1, ZS)])
        once[1] = added([half[span(PARTA + spot * CHUNK, CHUNK), :]] + [from_b[k] for k in range(1, PLANES)])
        stage(s, [(once.at[0], then_a.at[k], to) for k, to, _ in plane] + [(once.at[1], then_b.at[k], to) for k, to, _ in line])
        start_a = span(core * HALF + z * CHUNK, CHUNK)
        start_b = span(core * HALF + PARTA + spot * CHUNK, CHUNK)
        g_sum[s, start_a, :] = added([once[0]] + [then_a[k] for k in range(1, PLANES)])
        g_sum[s, start_b, :] = added([once[1]] + [then_b[k] for k in range(1, ZS)])
        here_a, here_b = g_sum.at[s, start_a, :], g_sum.at[s, start_b, :]
        stage(s, [(here_b, here_b, to) for _, to, _ in plane] + [(here_a, here_a, to) for _, to, _ in line])
        share = g_sum.at[s, span(core * HALF, HALF), :]
        stage(s, [(share, share, partner)])

    cuts = [0, 12, 16, 20, 24, 28, 31, 31]
    batches = [peers[i:j] for i, j in zip(cuts, cuts[1:])]
    send_slabs(0, peers)
    send_slabs(1, batches[0])
    for copy in local:
        copy.wait()
    wait_slabs(0, recv_sem)
    keep = [pltpu.make_async_copy(w_slab.at[s], w_out.at[s], keep_sem.at[s]) for s in range(SETS)]
    keep[0].start()
    correlate(0)
    total_light(0, batches[1:])
    wait_slabs(1, recv_sem)
    keep[1].start()
    correlate(1)
    total(1)
    for copy in used[0] + used[1]:
        copy.wait_send()
    for s in range(SETS):
        wait_slabs(s, send_sem)
    for copy in keep:
        copy.wait()


def finish_kernel(g_ref, w_ref, out_ref, g, x, a, m, u, slab, result, in_sem, out_sem):
    fetch = pltpu.make_async_copy(w_ref, slab, in_sem)
    fetch.start()
    g[...] = g_ref[:, :USED, :]
    factor(g, x, a, m, u)
    fetch.wait()
    stores = []
    tall = 2 * BLK
    for s in range(SETS):
        for i in range(NB // tall):
            lo, hi = tall * i, tall * i + tall
            inverse = x[s, lo:hi, :hi]
            head = inverse.astype(BF16)
            tail = (inverse - head.astype(F32)).astype(BF16)
            both = jnp.dot(jnp.concatenate([head, tail], axis=0), slab[s, :hi, :], preferred_element_type=F32)
            result[s, lo:hi, :] = both[:tall] + both[tall:]
            here = result.at[s, pl.ds(lo, tall), :]
            stores.append(pltpu.make_async_copy(here, out_ref.at[s, pl.ds(lo, tall), :], out_sem.at[s, i]))
            stores[-1].start()
    for store in stores:
        store.wait()


def per_device(orbitals, exchange_applied):
    width = orbitals.shape[2] // (YS * ZS)
    vmem = pl.BlockSpec(memory_space=pltpu.VMEM)
    anywhere = pl.BlockSpec(memory_space=pl.ANY)
    gram, slab = pl.pallas_call(
        exchange_kernel,
        out_shape=(
            jax.ShapeDtypeStruct((SETS, LROWS, BLK), F32),
            jax.ShapeDtypeStruct((SETS, NB, width), BF16),
        ),
        in_specs=[anywhere, anywhere],
        out_specs=(vmem, anywhere),
        scratch_shapes=[
            pltpu.VMEM((SETS, NB, width), BF16),
            pltpu.VMEM((SETS, NB, width), BF16),
            pltpu.VMEM((SETS, LROWS, BLK), F32),
            pltpu.VMEM((HALF, BLK), F32),
            pltpu.VMEM((2, CHUNK, BLK), F32),
            pltpu.VMEM((ZS, CHUNK, BLK), F32),
            pltpu.VMEM((PLANES, CHUNK, BLK), F32),
            pltpu.VMEM((PLANES, CHUNK, BLK), F32),
            pltpu.VMEM((ZS, CHUNK, BLK), F32),
            pltpu.VMEM((LHALF, BLK), F32),
            pltpu.VMEM((LPLANE, BLK), F32),
            pltpu.VMEM((PLANES, LPLANE, BLK), F32),
            pltpu.VMEM((ZS, LCHUNK, BLK), F32),
            pltpu.SemaphoreType.DMA((SETS, 2)),
            pltpu.SemaphoreType.DMA((SETS, 2)),
            pltpu.SemaphoreType.DMA((SETS, 2)),
            pltpu.SemaphoreType.DMA((SETS, MESSAGES)),
            pltpu.SemaphoreType.DMA((SETS, MESSAGES)),
            pltpu.SemaphoreType.DMA((SETS,)),
        ],
        compiler_params=pltpu.CompilerParams(collective_id=0, has_side_effects=True, vmem_limit_bytes=VMEM_LIMIT),
    )(orbitals, exchange_applied)
    return pl.pallas_call(
        finish_kernel,
        out_shape=jax.ShapeDtypeStruct((SETS, NB, width), F32),
        in_specs=[vmem, anywhere],
        out_specs=anywhere,
        scratch_shapes=[
            pltpu.VMEM((SETS, USED, BLK), F32),
            pltpu.VMEM((SETS, NB, NB), F32),
            pltpu.VMEM((BLK, 2 * BLK), F32),
            pltpu.VMEM((BLK, 2 * BLK), F32),
            pltpu.VMEM((SETS, BLK, NB), F32),
            pltpu.VMEM((SETS, NB, width), BF16),
            pltpu.VMEM((SETS, NB, width), F32),
            pltpu.SemaphoreType.DMA,
            pltpu.SemaphoreType.DMA((SETS, NBLK)),
        ],
        compiler_params=pltpu.CompilerParams(vmem_limit_bytes=VMEM_LIMIT),
    )(gram, slab)


def solution(mesh):
    placed = (P(None, "ga", "ba"), P(None, "ga", "ba"))
    return jax.shard_map(
        per_device,
        mesh=mesh,
        in_specs=placed,
        out_specs=P(None, None, ("ba", "ga")),
        check_vma=False,
    )
```

```python
import functools

import jax
import jax.numpy as jnp
from jax import lax
from jax.experimental import pallas as pl
from jax.experimental.pallas import tpu as pltpu
from jax.sharding import PartitionSpec as P

MESH = pl.DeviceIdType.MESH
F32 = jnp.float32
BF16 = jnp.bfloat16
NB, NG, SETS = 512, 294912, 2
BLK = 128
HB = BLK // 2
NBLK = NB // BLK
PANEL = 16
PAIRS = [(i, j) for i in range(NBLK) for j in range(i, NBLK)]
FIRST = [PAIRS.index((i, i)) for i in range(NBLK)]
USED = len(PAIRS) * BLK
GROWS = USED
LROWS = 16 * BLK
XS, YS, ZS = 4, 4, 8
HALF = GROWS // 2
PLANES = XS * YS
CHUNKA = 32
PARTA = CHUNKA * ZS
CHUNKB = (HALF - PARTA) // PLANES
LHALF = LROWS // 2
LPLANE = LHALF // PLANES
LCHUNK = LPLANE // ZS
MESSAGES = 2 + 3 * (PLANES - 1 + ZS - 1)
VMEM_LIMIT = 50 * 2**20

def ring(d, n):
    return min(d, n - d)


OFFSETS = sorted(
    [(dy, dz) for dy in range(YS) for dz in range(ZS) if (dy, dz) != (0, 0)],
    key=lambda t: ring(t[0], YS) + ring(t[1], ZS),
)


PLANE = sorted(
    [(dy, dx) for dy in range(YS) for dx in range(XS) if (dy, dx) != (0, 0)],
    key=lambda t: -ring(t[0], YS) - ring(t[1], XS),
)


def pieces(a):
    head = a.astype(BF16)
    rest = a - head.astype(F32)
    middle = rest.astype(BF16)
    return head, middle, (rest - middle.astype(F32)).astype(BF16)


def stacked(left, right, axis_left, axis_right):
    a, b = pieces(left), pieces(right)
    order = ((0, 0), (0, 1), (1, 0), (1, 1), (0, 2), (2, 0))
    return lax.dot_general(
        jnp.concatenate([a[i] for i, _ in order], axis=axis_left),
        jnp.concatenate([b[j] for _, j in order], axis=axis_right),
        (((axis_left,), (axis_right,)), ((), ())),
        preferred_element_type=F32,
    )


def tn(a, b):
    return stacked(a, b, 0, 0)


def nn(a, b):
    return stacked(a, b, 1, 0)


def nt(a, b):
    return lax.dot_general(a, b, (((1,), (1,)), ((), ())), preferred_element_type=F32)


def pack(first, second):
    return jnp.concatenate([first[:, :HB], second[:, :HB], first[:, HB:], second[:, HB:]], axis=1)


def unpack(packed):
    return (
        jnp.concatenate([packed[:, :HB], packed[:, BLK : BLK + HB]], axis=1),
        jnp.concatenate([packed[:, HB:BLK], packed[:, BLK + HB :]], axis=1),
    )


def factor_blocks(a_ref, x_ref):
    wide = (8, BLK)
    sub = lax.broadcasted_iota(jnp.int32, wide, 0)
    left = lax.broadcasted_iota(jnp.int32, wide, 1) < HB
    rows = lax.broadcasted_iota(jnp.int32, (BLK, 2 * BLK), 0)
    cols = lax.broadcasted_iota(jnp.int32, (BLK, 2 * BLK), 1)
    x_ref[...] = jnp.where(rows == cols % HB + cols // BLK * HB, 1.0, 0.0).astype(F32)
    own = PANEL // 8
    for base in range(0, BLK, PANEL):
        v = own if base + PANEL == BLK else 2 * own
        at = [slice(base + 8 * i, base + 8 * i + 8) for i in range(v)]
        t = [[a_ref[at[i], :BLK], a_ref[at[i], BLK:], x_ref[at[i], :BLK], x_ref[at[i], BLK:]] for i in range(v)]
        side, first = divmod(base, HB)
        c = [
            [
                jnp.where(
                    left,
                    jnp.broadcast_to(t[i][side][:, first + r : first + r + 1], wide),
                    jnp.broadcast_to(t[i][side][:, HB + first + r : HB + first + r + 1], wide),
                )
                for i in range(v)
            ]
            for r in range(PANEL)
        ]
        live = [k for k in range(4) if not (k == 0 and side == 1) and not (k == 3 and side == 0 and base + 2 * PANEL <= HB)]
        d = [jnp.ones(wide, F32) for _ in range(own)]
        for r in range(PANEL):
            h, q = divmod(r, 8)
            pivot = jnp.broadcast_to(c[r][h][q : q + 1, :], wide)
            inv = 1.0 / pivot
            d[h] = jnp.where(sub == q, pivot, d[h])
            trow = {k: jnp.broadcast_to(t[h][k][q : q + 1, :], wide) for k in live}
            crow = {j: jnp.broadcast_to(c[j][h][q : q + 1, :], wide) for j in range(r + 1, PANEL)}
            for i in range(h, v):
                if i == h and q == 7:
                    continue
                m = c[r][i] * inv
                if i == h:
                    m = jnp.where(sub > q, m, 0.0)
                for j in range(r + 1, PANEL):
                    c[j][i] = c[j][i] - m * crow[j]
                for k in live:
                    t[i][k] = t[i][k] - m * trow[k]
        for i in range(own):
            s = lax.rsqrt(d[i])
            t[i] = [e * s for e in t[i]]
        for i in range(v):
            a_ref[at[i], :BLK], a_ref[at[i], BLK:], x_ref[at[i], :BLK], x_ref[at[i], BLK:] = t[i]
        rest = base + 2 * PANEL
        if rest < BLK:
            u = a_ref[base : base + PANEL, :]
            w = x_ref[base : base + PANEL, :]
            both = jnp.concatenate([u, w], axis=1)
            for lo in (0, HB):
                if rest >= lo + HB:
                    continue
                skip = max(rest - lo, 0)
                p = tn(u[:, 2 * lo : 2 * lo + BLK], both)
                pick = lax.broadcasted_iota(jnp.int32, (HB - skip, 4 * BLK), 1) % BLK < HB
                update = jnp.where(pick, p[skip:HB], p[HB + skip :])
                if lo == 0 or rest <= HB:
                    a_ref[lo + skip : lo + HB, :] = a_ref[lo + skip : lo + HB, :] - update[:, : 2 * BLK]
                else:
                    a_ref[lo + skip : lo + HB, BLK:] = a_ref[lo + skip : lo + HB, BLK:] - update[:, BLK : 2 * BLK]
                x_ref[lo + skip : lo + HB, :] = x_ref[lo + skip : lo + HB, :] - update[:, 2 * BLK :]


def factor(g_ref, x_ref, a_ref, m_ref, u_ref):
    def block(i, j):
        at = (FIRST[i] + j - i) * BLK
        return slice(at, at + BLK)

    x_ref[...] = jnp.zeros((SETS, NB, NB), F32)

    def step(k, carry):
        diagonal = pl.ds(pl.multiple_of(k * (2 * NBLK + 1 - k) // 2 * BLK, BLK), BLK)
        a_ref[...] = pack(g_ref[0, diagonal, :], g_ref[1, diagonal, :])
        factor_blocks(a_ref, m_ref)
        ms = unpack(m_ref[...])
        for kk in range(NBLK):
            @pl.when(k == kk)
            def _():
                lo, hi = BLK * kk, BLK * kk + BLK
                below = NB - hi
                for s, m in enumerate(ms):
                    x_ref[s, lo:hi, lo:hi] = m
                    right = [g_ref[s, block(kk, j), :] for j in range(kk + 1, NBLK)]
                    left = [x_ref[s, lo:hi, :lo]] if kk else []
                    row = nn(m, jnp.concatenate(right + left, axis=1))
                    if below:
                        u_ref[s, :, hi:] = row[:, :below]
                    if kk:
                        x_ref[s, lo:hi, :lo] = row[:, below:]
                if below:
                    for s in range(SETS):
                        u = u_ref[s, :, hi:]
                        update = nn(u.T, jnp.concatenate([u, x_ref[s, lo:hi, :hi]], axis=1))
                        for i in range(kk + 1, NBLK):
                            at = slice(BLK * i - hi, BLK * i - hi + BLK)
                            for j in range(i, NBLK):
                                g_ref[s, block(i, j), :] = g_ref[s, block(i, j), :] - update[at, BLK * j - hi : BLK * j - hi + BLK]
                            li = BLK * i
                            x_ref[s, li : li + BLK, :hi] = x_ref[s, li : li + BLK, :hi] - update[at, below:]
        return carry

    lax.fori_loop(0, NBLK, step, 0)


def exchange_kernel(
    o_ref, w_ref, g_sum, w_out, o_slab, w_slab, part, half, once, from_a, from_b, then_a, then_b, light, middle, from_p, from_q,
    send_sem, recv_sem, own_sem, out_sem, in_sem, keep_sem
):
    ga, ba = lax.axis_index("ga"), lax.axis_index("ba")
    y, z = ga // ZS, lax.rem(ga, ZS)
    x, core = ba // 2, lax.rem(ba, 2)

    def device(x, y, z, core):
        return (y * ZS + z, x * 2 + core)

    def ahead(i, k, n):
        return lax.rem(i + k, n)

    def span(start, size):
        return pl.ds(pl.multiple_of(start, 8), size)

    peers = [device(x, ahead(y, dy, YS), ahead(z, dz, ZS), core) for dy, dz in OFFSETS]
    partner = device(x, y, z, 1 - core)
    line = [(k, device(x, y, ahead(z, k, ZS), core), ahead(z, k, ZS)) for k in range(1, ZS)]
    plane = [
        (dy * XS + dx, device(ahead(x, dx, XS), ahead(y, dy, YS), z, core), ahead(y, dy, YS) * XS + ahead(x, dx, XS))
        for dy, dx in PLANE
    ]
    spot = y * XS + x
    greeted = [*peers, partner, *(to for (dy, dx), (_, to, _) in zip(PLANE, plane) if dx)]
    barrier = pltpu.get_barrier_semaphore()
    for p in greeted:
        pl.semaphore_signal(barrier, inc=1, device_id=p, device_id_type=MESH)
    width = o_slab.shape[2]
    rows = o_ref.shape[1]
    mine = pl.ds(pl.multiple_of(ga * rows, rows), rows)
    own = pl.ds(pl.multiple_of(ga * width, BLK), width)
    arrays = ((o_ref, o_slab), (w_ref, w_slab))
    local = [
        pltpu.make_async_copy(src.at[s, :, own], dst.at[s, mine, :], own_sem.at[s, a])
        for s in range(SETS)
        for a, (src, dst) in enumerate(arrays)
    ]
    for copy in local:
        copy.start()
    part[:, USED:, :] = jnp.zeros((SETS, LROWS - USED, BLK), F32)
    pl.semaphore_wait(barrier, len(greeted))

    def send_slabs(s, chosen):
        for p in chosen:
            columns = pl.ds(pl.multiple_of(p[0] * width, BLK), width)
            for a, (src, dst) in enumerate(arrays):
                pltpu.make_async_remote_copy(
                    src_ref=src.at[s, :, columns],
                    dst_ref=dst.at[s, mine, :],
                    send_sem=send_sem.at[s, a],
                    recv_sem=recv_sem.at[s, a],
                    device_id=p,
                    device_id_type=MESH,
                ).start()

    def wait_slabs(s, sem):
        for a, (src, dst) in enumerate(arrays):
            all_but_one = dst.at[s, pl.ds(0, len(peers) * rows), :]
            pltpu.make_async_copy(all_but_one, all_but_one, sem.at[s, a]).wait()

    def correlate(s):
        for i in range(0, NBLK, 2):
            lo, hi = BLK * i, BLK * (i + 2)
            product = nt(o_slab[s, lo:hi, :], w_slab[s, lo:, :]) + nt(w_slab[s, lo:hi, :], o_slab[s, lo:, :])
            for k in range(i, i + 2):
                for j in range(k, NBLK):
                    at = (FIRST[k] + j - k) * BLK
                    block = product[(k - i) * BLK : (k - i + 1) * BLK, (j - i) * BLK : (j - i + 1) * BLK]
                    part[s, at : at + BLK, :] = block * (-0.5 / NG)

    used = [[], []]

    def stage(s, transfers, between=None):
        copies = [
            pltpu.make_async_remote_copy(
                src_ref=src, dst_ref=dst, send_sem=out_sem.at[s, at], recv_sem=in_sem.at[s, at], device_id=to, device_id_type=MESH
            )
            for at, (src, dst, to) in enumerate(transfers, len(used[s]))
        ]
        for copy in copies:
            copy.start()
        if between is not None:
            send_slabs(1, between)
        for copy in copies:
            copy.wait_recv()
        used[s].extend(copies)

    def added(terms):
        while len(terms) > 1:
            terms = [sum(terms[i : i + 2][1:], terms[i]) for i in range(0, len(terms), 2)]
        return terms[0]

    def total_light(s, batches):
        stage(s, [(part.at[s, span((1 - core) * LHALF, LHALF), :], light, partner)], batches[0])
        light[...] = light[...] + part[s, span(core * LHALF, LHALF), :]
        stage(s, [(light.at[span(i * LPLANE, LPLANE), :], from_p.at[k], to) for k, to, i in plane], batches[1])
        middle[...] = added([light[span(spot * LPLANE, LPLANE), :]] + [from_p[k] for k in range(1, PLANES)])
        stage(s, [(middle.at[span(i * LCHUNK, LCHUNK), :], from_q.at[k], to) for k, to, i in line], batches[2])
        start = core * LHALF + spot * LPLANE
        here = span(start + z * LCHUNK, LCHUNK)
        g_sum[s, here, :] = added([middle[span(z * LCHUNK, LCHUNK), :]] + [from_q[k] for k in range(1, ZS)])
        for batch, done, to_all in (
            (batches[3], g_sum.at[s, here, :], [to for _, to, _ in line]),
            (batches[4], g_sum.at[s, span(start, LPLANE), :], [to for _, to, _ in plane]),
            (batches[5], g_sum.at[s, span(core * LHALF, LHALF), :], [partner]),
        ):
            stage(s, [(done, done, to) for to in to_all], batch)

    def total(s):
        stage(s, [(part.at[s, span((1 - core) * HALF, HALF), :], half, partner)])
        half[...] = half[...] + part[s, span(core * HALF, HALF), :]
        stage(
            s,
            [(half.at[span(PARTA + i * CHUNKB, CHUNKB), :], from_b.at[k], to) for k, to, i in plane]
            + [(half.at[span(i * CHUNKA, CHUNKA), :], from_a.at[k], to) for k, to, i in line],
        )
        once[0] = added([half[span(z * CHUNKA, CHUNKA), :]] + [from_a[k] for k in range(1, ZS)])
        once[1, :CHUNKB] = added([half[span(PARTA + spot * CHUNKB, CHUNKB), :]] + [from_b[k] for k in range(1, PLANES)])
        stage(s, [(once.at[0], then_a.at[k], to) for k, to, _ in plane] + [(once.at[1, pl.ds(0, CHUNKB), :], then_b.at[k], to) for k, to, _ in line])
        start_a = span(core * HALF + z * CHUNKA, CHUNKA)
        start_b = span(core * HALF + PARTA + spot * CHUNKB, CHUNKB)
        g_sum[s, start_a, :] = added([once[0]] + [then_a[k] for k in range(1, PLANES)])
        g_sum[s, start_b, :] = added([once[1, :CHUNKB]] + [then_b[k] for k in range(1, ZS)])
        here_a, here_b = g_sum.at[s, start_a, :], g_sum.at[s, start_b, :]
        stage(s, [(here_b, here_b, to) for _, to, _ in plane] + [(here_a, here_a, to) for _, to, _ in line])
        share = g_sum.at[s, span(core * HALF, HALF), :]
        stage(s, [(share, share, partner)])

    cuts = [0, 12, 16, 20, 24, 28, 31, 31]
    batches = [peers[i:j] for i, j in zip(cuts, cuts[1:])]
    send_slabs(0, peers)
    send_slabs(1, batches[0])
    for copy in local:
        copy.wait()
    wait_slabs(0, recv_sem)
    keep = [pltpu.make_async_copy(w_slab.at[s], w_out.at[s], keep_sem.at[s]) for s in range(SETS)]
    keep[0].start()
    correlate(0)
    total_light(0, batches[1:])
    wait_slabs(1, recv_sem)
    keep[1].start()
    correlate(1)
    total(1)
    for copy in used[0] + used[1]:
        copy.wait_send()
    for s in range(SETS):
        wait_slabs(s, send_sem)
    for copy in keep:
        copy.wait()


def finish_kernel(g_ref, w_ref, out_ref, g, x, a, m, u, slab, result, in_sem, out_sem):
    fetch = pltpu.make_async_copy(w_ref, slab, in_sem)
    fetch.start()
    g[...] = g_ref[:, :USED, :]
    factor(g, x, a, m, u)
    fetch.wait()
    stores = []
    tall = 2 * BLK
    for s in range(SETS):
        for i in range(NB // tall):
            lo, hi = tall * i, tall * i + tall
            inverse = x[s, lo:hi, :hi]
            head = inverse.astype(BF16)
            tail = (inverse - head.astype(F32)).astype(BF16)
            both = jnp.dot(jnp.concatenate([head, tail], axis=0), slab[s, :hi, :], preferred_element_type=F32)
            result[s, lo:hi, :] = both[:tall] + both[tall:]
            here = result.at[s, pl.ds(lo, tall), :]
            stores.append(pltpu.make_async_copy(here, out_ref.at[s, pl.ds(lo, tall), :], out_sem.at[s, i]))
            stores[-1].start()
    for store in stores:
        store.wait()


def per_device(orbitals, exchange_applied):
    width = orbitals.shape[2] // (YS * ZS)
    vmem = pl.BlockSpec(memory_space=pltpu.VMEM)
    anywhere = pl.BlockSpec(memory_space=pl.ANY)
    gram, slab = pl.pallas_call(
        exchange_kernel,
        out_shape=(
            jax.ShapeDtypeStruct((SETS, LROWS, BLK), F32),
            jax.ShapeDtypeStruct((SETS, NB, width), BF16),
        ),
        in_specs=[anywhere, anywhere],
        out_specs=(vmem, anywhere),
        scratch_shapes=[
            pltpu.VMEM((SETS, NB, width), BF16),
            pltpu.VMEM((SETS, NB, width), BF16),
            pltpu.VMEM((SETS, LROWS, BLK), F32),
            pltpu.VMEM((HALF, BLK), F32),
            pltpu.VMEM((2, CHUNKA, BLK), F32),
            pltpu.VMEM((ZS, CHUNKA, BLK), F32),
            pltpu.VMEM((PLANES, CHUNKB, BLK), F32),
            pltpu.VMEM((PLANES, CHUNKA, BLK), F32),
            pltpu.VMEM((ZS, CHUNKB, BLK), F32),
            pltpu.VMEM((LHALF, BLK), F32),
            pltpu.VMEM((LPLANE, BLK), F32),
            pltpu.VMEM((PLANES, LPLANE, BLK), F32),
            pltpu.VMEM((ZS, LCHUNK, BLK), F32),
            pltpu.SemaphoreType.DMA((SETS, 2)),
            pltpu.SemaphoreType.DMA((SETS, 2)),
            pltpu.SemaphoreType.DMA((SETS, 2)),
            pltpu.SemaphoreType.DMA((SETS, MESSAGES)),
            pltpu.SemaphoreType.DMA((SETS, MESSAGES)),
            pltpu.SemaphoreType.DMA((SETS,)),
        ],
        compiler_params=pltpu.CompilerParams(collective_id=0, has_side_effects=True, vmem_limit_bytes=VMEM_LIMIT),
    )(orbitals, exchange_applied)
    return pl.pallas_call(
        finish_kernel,
        out_shape=jax.ShapeDtypeStruct((SETS, NB, width), F32),
        in_specs=[vmem, anywhere],
        out_specs=anywhere,
        scratch_shapes=[
            pltpu.VMEM((SETS, USED, BLK), F32),
            pltpu.VMEM((SETS, NB, NB), F32),
            pltpu.VMEM((BLK, 2 * BLK), F32),
            pltpu.VMEM((BLK, 2 * BLK), F32),
            pltpu.VMEM((SETS, BLK, NB), F32),
            pltpu.VMEM((SETS, NB, width), BF16),
            pltpu.VMEM((SETS, NB, width), F32),
            pltpu.SemaphoreType.DMA,
            pltpu.SemaphoreType.DMA((SETS, NBLK)),
        ],
        compiler_params=pltpu.CompilerParams(vmem_limit_bytes=VMEM_LIMIT),
    )(gram, slab)


def solution(mesh):
    placed = (P(None, "ga", "ba"), P(None, "ga", "ba"))
    return jax.shard_map(
        per_device,
        mesh=mesh,
        in_specs=placed,
        out_specs=P(None, None, ("ba", "ga")),
        check_vma=False,
    )
```
